32 devices in a mesh: expert: 8 (over z, y), head: 4 (over x, core).
Axes of the slice: x: 2, y: 2, z: 4, core: 2. Of those that a mesh axis runs over, the one named last changes fastest.
Arguments:
- block_input: bfloat16 [25216, 768], P(('expert', 'head')), may hold values from -6 to 6
- output_grad: bfloat16 [25216, 768], P(('expert', 'head')), may hold values from -6 to 6
- routes: int32 [25216, 2], P(('expert', 'head')), may hold values from 0 to 7, all different within a row; in each aligned block of 788 rows (0 to 787, 788 to 1575, ...) at most 316 rows name the same one
- qkv_master: float32 [768, 2304], P(('expert', 'head')), may hold values from -0.21875 to 0.21875
- qkv_mean: float32 [768, 2304], P(('expert', 'head')), may hold values from -512 to 512
- qkv_square: float32 [768, 2304], P(('expert', 'head')), may hold values from 4538.88 to 36311.04
- proj_master: float32 [768, 768], P(('expert', 'head')), may hold values from -0.875 to 0.875
- proj_mean: float32 [768, 768], P(('expert', 'head')), may hold values from -160 to 160
- proj_square: float32 [768, 768], P(('expert', 'head')), may hold values from 322.7648 to 2521.6
- router_master: float32 [768, 8], P(('expert', 'head')), may hold values from -0.109375 to 0.109375
- router_mean: float32 [768, 8], P(('expert', 'head')), may hold values from -4096 to 4096
- router_square: float32 [768, 8], P(('expert', 'head')), may hold values from 217866.23 to 1742929.9
- norm_master: float32 [4, 768], P(None, ('expert', 'head')), may hold values from -0.6 to 1.6
- norm_mean: float32 [4, 768], P(None, ('expert', 'head')), may hold values from -640 to 640
- norm_square: float32 [4, 768], P(None, ('expert', 'head')), may hold values from 6304 to 50432
- inner_master: float32 [8, 768, 3072], P('expert', None, 'head'), may hold values from -0.21875 to 0.21875
- inner_mean: float32 [8, 768, 3072], P('expert', None, 'head'), may hold values from -64 to 64
- inner_square: float32 [8, 768, 3072], P('expert', None, 'head'), may hold values from 70.92 to 567.36
- outer_master: float32 [8, 3072, 768], P('expert', 'head'), may hold values from -0.4375 to 0.4375
- outer_mean: float32 [8, 3072, 768], P('expert', 'head'), may hold values from -32 to 32
- outer_square: float32 [8, 3072, 768], P('expert', 'head'), may hold values from 17.73 to 141.84
Outputs:
- block_output: bfloat16 [25216, 768], P(('expert', 'head'))
- input_grad: float32 [25216, 768], P(('expert', 'head'))
- qkv_weight: float32 [768, 2304], P(('expert', 'head'))
- qkv_momentum: float32 [768, 2304], P(('expert', 'head'))
- qkv_variance: float32 [768, 2304], P(('expert', 'head'))
- qkv_copy: bfloat16 [768, 2304], P(('expert', 'head'))
- proj_weight: float32 [768, 768], P(('expert', 'head'))
- proj_momentum: float32 [768, 768], P(('expert', 'head'))
- proj_variance: float32 [768, 768], P(('expert', 'head'))
- proj_copy: bfloat16 [768, 768], P(('expert', 'head'))
- router_weight: float32 [768, 8], P(('expert', 'head'))
- router_momentum: float32 [768, 8], P(('expert', 'head'))
- router_variance: float32 [768, 8], P(('expert', 'head'))
- router_copy: bfloat16 [768, 8], P(('expert', 'head'))
- norm_weight: float32 [4, 768], P(None, ('expert', 'head'))
- norm_momentum: float32 [4, 768], P(None, ('expert', 'head'))
- norm_variance: float32 [4, 768], P(None, ('expert', 'head'))
- norm_copy: bfloat16 [4, 768], P(None, ('expert', 'head'))
- inner_weight: float32 [8, 768, 3072], P('expert', None, 'head')
- inner_momentum: float32 [8, 768, 3072], P('expert', None, 'head')
- inner_variance: float32 [8, 768, 3072], P('expert', None, 'head')
- inner_copy: bfloat16 [8, 768, 3072], P('expert', None, 'head')
- outer_weight: float32 [8, 3072, 768], P('expert', 'head')
- outer_momentum: float32 [8, 3072, 768], P('expert', 'head')
- outer_variance: float32 [8, 3072, 768], P('expert', 'head')
- outer_copy: bfloat16 [8, 3072, 768], P('expert', 'head')
The draws below stay inside these ranges and needn't reach their ends.
Inputs may be any that keep to these rules, and one draw needn't show every extreme that they name: `routes`: in the rows of one device (aligned blocks of 788 rows) no expert is named more than 316 times, a bound that some block reaches; a row names two different experts.
All inputs are finite; a program needn't handle non-finite values.
Results may differ from the reference program's by a relative error of at most 0.017.
Values may be sent and summed in bfloat16 or wider, within the bound.
A program may use at most 320 MiB of HBM per device.

```python
import math
import jax
import jax.numpy as jnp
import numpy as np
from jax import lax

D = 768
HEADS = 12
HD = 64
FF = 3072
SEQ = 197
IMG_DEV = 4
TOP = 2
STEP = 3
TOK_DEV = 788
TOKENS = 25216
EXPERTS = 8
CAP = 316
SLOTS = 10112
N_HEAD = 4
DEVICES = 32


def draw_norm_master(key, part):
    key = jax.random.fold_in(key, 17)
    gain_key, shift_key = jax.random.split(key)
    gains = jnp.exp(jax.random.uniform(gain_key, (2, D), jnp.float32, -0.5, 0.45))
    shifts = 0.2 * jax.random.truncated_normal(shift_key, -3.0, 3.0, (2, D), jnp.float32)
    return jnp.stack([gains[0], shifts[0], gains[1], shifts[1]], axis=0)


def block_levels(key, dims, cuts, least, largest):
    level = 1.0
    for axis_at, shards_of in cuts:
        steps = jax.random.uniform(jax.random.fold_in(jax.random.fold_in(key, 6), axis_at), (shards_of,), jnp.float32, least / len(cuts), largest / len(cuts))
        level = level * jnp.repeat(jnp.exp(steps), dims[axis_at] // shards_of).reshape((-1,) + (1,) * (len(dims) - 1 - axis_at))
    return level


def shared_out(own_key, own, number, rows, amount, top, limit, slope):
    order = jax.random.permutation(own_key, amount)
    heavy_load, common = shares(amount, rows * top, limit, slope, True), shares(amount, rows * top, limit, slope, False)
    places = jnp.arange(amount)

    def named(sizes, offset_by):
        used = int((sizes > 0).sum())
        fixed = max(1, used // 4)
        passed = fixed + (places - fixed + offset_by * (used - fixed)) % max(1, amount - fixed)
        return jnp.zeros((amount,), jnp.int32).at[order[jnp.where(places < fixed, places, passed)]].set(jnp.asarray(sizes, jnp.int32))

    sizes = jnp.where(number % 4 == 0, named(heavy_load, number // 4), named(common, number - number // 4 - 1))
    mixed = jax.random.permutation(jax.random.fold_in(own, 3), amount)
    donor, receiver = mixed[0:amount // 2 * 2:2], mixed[1:amount // 2 * 2:2]
    room = jnp.minimum(sizes[donor] - 1, limit - sizes[receiver]) // 2
    room = jnp.where((donor == order[0]) | (receiver == order[0]) | (sizes[receiver] == 0), 0, jnp.maximum(room, 0))
    passed = jax.random.randint(jax.random.fold_in(own, 4), (amount // 2,), 0, 1 << 20) % (room + 1)
    sizes = sizes.at[donor].add(-passed).at[receiver].add(passed)
    labels = jnp.searchsorted(jnp.cumsum(sizes), jnp.arange(rows * top), side="right").astype(jnp.int32)
    grid = labels.reshape(top, rows).T
    grid = grid[jax.random.permutation(jax.random.fold_in(own, 1), rows)]
    offset_by = jax.random.randint(jax.random.fold_in(own, 2), (rows, 1), 0, top)
    return jnp.take_along_axis(grid, (jnp.arange(top)[None, :] + offset_by) % top, axis=1)


def shares(number_of, total, most, skew, full):
    weights = [(1 << 20) // math.isqrt(grade ** skew) + 1 for grade in range(1, number_of + 1)]
    largest = most if full else min(most, max(-(-total // number_of), total * weights[0] // sum(weights)))
    least = 1 if total - largest >= number_of - 1 else 0
    counts, spare = [largest] + [least] * (number_of - 1), total - largest - least * (number_of - 1)
    while spare > 0:
        free = [i for i in range(1, number_of) if counts[i] < largest] or [i for i in range(1, number_of) if counts[i] < most]
        mass, budget = sum([weights[i] for i in free]), spare
        for i in free:
            more = min(most - counts[i], max(1, budget * weights[i] // mass), spare)
            counts[i] = counts[i] + more
            spare = spare - more
    return np.array(counts)


def scatter_about(key, shape, width, limit, shards=(), held_as=jnp.bfloat16):
    loudness = block_levels(key, shape, shards, -0.22, 0.18) if shards else 1.0
    values = jax.random.normal(key, shape, jnp.float32) * width * loudness
    return jnp.minimum(jnp.maximum(values, -limit), limit).astype(held_as)


def setup_inputs(seed: int = 0) -> dict:
    keys = jax.random.split(jax.random.key(seed), 22)
    block_input = scatter_about(keys[0], (TOKENS, D), 1.0, 6.0, ((0, 32),))
    output_grad = scatter_about(keys[1], (TOKENS, D), 1.0, 6.0, ((0, 32),))
    routes_keys = jax.random.split(jax.random.fold_in(keys[2], 1), TOKENS // TOK_DEV)
    routes_turns = jax.random.permutation(jax.random.fold_in(keys[2], 3), TOKENS // TOK_DEV)
    routes = jax.vmap(lambda own, number: shared_out(jax.random.fold_in(keys[2], 2), own, number, TOK_DEV, EXPERTS, TOP, CAP, 1))(routes_keys, routes_turns).reshape((TOKENS, TOP))
    qkv_master = scatter_about(keys[3], (D, 3 * D), D ** -0.5, 0.21875, ((0, 32),), jnp.float32)
    qkv_mean = scatter_about(keys[4], (D, 3 * D), (0.6 * TOKENS ** 0.5), 512.0, ((0, 32),), jnp.float32)
    qkv_square = jnp.clip(jnp.exp(math.log(36311.04) - 2.0794415 * jax.random.uniform(keys[5], (D, 3 * D), jnp.float32) ** block_levels(keys[5], (D, 3 * D), ((0, 32),), -0.2, 0.2)), 4538.88, 36311.04)
    proj_master = scatter_about(keys[6], (D, D), (D // 16) ** -0.5, 0.875, ((0, 32),), jnp.float32)
    proj_mean = scatter_about(keys[7], (D, D), (0.16 * TOKENS ** 0.5), 160.0, ((0, 32),), jnp.float32)
    proj_square = jnp.clip(jnp.exp(math.log(2521.6) - 2.055725 * jax.random.uniform(keys[8], (D, D), jnp.float32) ** block_levels(keys[8], (D, D), ((0, 32),), -0.2, 0.2)), 322.7648, 2521.6)
    router_master = scatter_about(keys[9], (D, EXPERTS), (4 * D) ** -0.5, 0.109375, ((0, 32),), jnp.float32)
    router_mean = scatter_about(keys[10], (D, EXPERTS), (0.42 * (D * TOKENS // EXPERTS) ** 0.5), 4096.0, ((0, 32),), jnp.float32)
    router_square = jnp.clip(jnp.exp(math.log(1742929.9) - 2.0794415 * jax.random.uniform(keys[11], (D, EXPERTS), jnp.float32) ** block_levels(keys[11], (D, EXPERTS), ((0, 32),), -0.2, 0.2)), 217866.23, 1742929.9)
    norm_master = draw_norm_master(jax.random.fold_in(keys[21], 71), 0)
    norm_mean = scatter_about(keys[13], (4, D), (0.7 * TOKENS ** 0.5), 640.0, ((1, 32),), jnp.float32)
    norm_square = jnp.clip(jnp.exp(math.log(50432.0) - 2.0794415 * jax.random.uniform(keys[14], (4, D), jnp.float32) ** block_levels(keys[14], (4, D), ((1, 32),), -0.2, 0.2)), 6304.0, 50432.0)
    inner_master = scatter_about(keys[15], (EXPERTS, D, FF), D ** -0.5, 0.21875, ((0, 8), (2, 4)), jnp.float32)
    inner_mean = scatter_about(keys[16], (EXPERTS, D, FF), (0.21 * (TOKENS // EXPERTS) ** 0.5), 64.0, ((0, 8), (2, 4)), jnp.float32)
    inner_square = jnp.clip(jnp.exp(math.log(567.36) - 2.0794415 * jax.random.uniform(keys[17], (EXPERTS, D, FF), jnp.float32) ** block_levels(keys[17], (EXPERTS, D, FF), ((0, 8), (2, 4)), -0.2, 0.2)), 70.92, 567.36)
    outer_master = scatter_about(keys[18], (EXPERTS, FF, D), (max(1, FF * 4 // (EXPERTS * EXPERTS))) ** -0.5, 0.4375, ((0, 8), (1, 4)), jnp.float32)
    outer_mean = scatter_about(keys[19], (EXPERTS, FF, D), (0.85 * (TOKENS // EXPERTS) ** 0.5 * EXPERTS ** -1), 32.0, ((0, 8), (1, 4)), jnp.float32)
    outer_square = jnp.clip(jnp.exp(math.log(141.84) - 2.0794415 * jax.random.uniform(keys[20], (EXPERTS, FF, D), jnp.float32) ** block_levels(keys[20], (EXPERTS, FF, D), ((0, 8), (1, 4)), -0.2, 0.2)), 17.73, 141.84)
    return dict(block_input=block_input, output_grad=output_grad, routes=routes, qkv_master=qkv_master, qkv_mean=qkv_mean, qkv_square=qkv_square, proj_master=proj_master, proj_mean=proj_mean, proj_square=proj_square, router_master=router_master, router_mean=router_mean, router_square=router_square, norm_master=norm_master, norm_mean=norm_mean, norm_square=norm_square, inner_master=inner_master, inner_mean=inner_mean, inner_square=inner_square, outer_master=outer_master, outer_mean=outer_mean, outer_square=outer_square)


EPS_NORM = 1e-06
BETA_ONE = 0.5
BETA_TWO = 0.5
EPS_ADAM = 1e-08
DECAY = 0.1
NORM_RATE = 0.3

@jax.custom_vjp
def low(v):
    return lax.optimization_barrier(v.astype(jnp.bfloat16)).astype(jnp.float32)

@jax.custom_vjp
def low_back(v):
    return v

def low_keep(v):
    return (low(v), None)

def low_pass(kept, grad):
    return (grad,)

def back_keep(v):
    return (v, None)

def back_low(kept, grad):
    return (low(grad),)
low.defvjp(low_keep, low_pass)
low_back.defvjp(back_keep, back_low)

def highest(left, right):
    return jnp.dot(left, right, precision=lax.Precision.HIGHEST, preferred_element_type=jnp.float32)

def layer_norm(values, gain_row, shift_row):
    centered = values - lax.optimization_barrier(jnp.mean(values, axis=-1, keepdims=True))
    spread = lax.rsqrt(lax.optimization_barrier(jnp.mean(centered * centered, axis=-1, keepdims=True)) + EPS_NORM)
    return centered * spread * gain_row + shift_row

def gelu_tanh(values):
    return jax.nn.gelu(values, approximate=True)

def adam_step(master, first_state, square, gradient, step_rate):
    momentum = BETA_ONE * first_state + (1.0 - BETA_ONE) * gradient
    variance = BETA_TWO * square + (1.0 - BETA_TWO) * gradient * gradient
    first_fix = momentum / (1.0 - BETA_ONE ** STEP)
    second_fix = variance / (1.0 - BETA_TWO ** STEP)
    updated = master - step_rate * (first_fix / (jnp.sqrt(second_fix) + EPS_ADAM) + DECAY * master)
    return (updated, momentum, variance, updated.astype(jnp.bfloat16))

def reference(block_input, output_grad, routes, qkv_master, qkv_mean, qkv_square, proj_master, proj_mean, proj_square, router_master, router_mean, router_square, norm_master, norm_mean, norm_square, inner_master, inner_mean, inner_square, outer_master, outer_mean, outer_square):
    pair_expert = routes.reshape(-1)
    onehot = (pair_expert[:, None] == jnp.arange(EXPERTS, dtype=jnp.int32)[None, :]).astype(jnp.int32)
    before = jnp.cumsum(onehot, axis=0) - onehot
    position = lax.optimization_barrier(jnp.sum(before * onehot, axis=1))
    target = pair_expert * SLOTS + position
    source = jnp.full((EXPERTS * SLOTS,), TOKENS, jnp.int32).at[target].set(jnp.arange(2 * TOKENS, dtype=jnp.int32) // 2)
    choose = (routes[:, :, None] == jnp.arange(EXPERTS, dtype=jnp.int32)[None, None, :]).astype(jnp.float32)
    score_scale = HD ** (-0.5)
    slice_width = FF // N_HEAD

    def forward(inputs, qkv_full, proj_full, router_full, norm_full, inner_full, outer_full):
        normed = low(layer_norm(inputs, norm_full[0], norm_full[1]))

        def attend(image_block):
            qkv_rows = low_back(low(highest(image_block, qkv_full)))
            qkv_rows = qkv_rows.reshape(IMG_DEV, SEQ, HEADS, 3, HD)
            query_rows = qkv_rows[:, :, :, 0]
            key_rows = qkv_rows[:, :, :, 1]
            value_rows = qkv_rows[:, :, :, 2]
            scores = low_back(jnp.einsum('bqhd,bkhd->bhqk', query_rows, key_rows, precision=lax.Precision.HIGHEST)) * score_scale
            row_max = lax.optimization_barrier(jnp.max(scores, axis=-1, keepdims=True))
            expo = jnp.exp(scores - row_max)
            prob_rows = low(expo / lax.optimization_barrier(jnp.sum(expo, axis=-1, keepdims=True)))
            attended = jnp.einsum('bhqk,bkhd->bqhd', prob_rows, value_rows, precision=lax.Precision.HIGHEST)
            attended = low_back(low(attended)).reshape(TOK_DEV, D)
            return low_back(highest(attended, proj_full))
        attention = lax.map(jax.checkpoint(attend), normed.reshape(DEVICES, TOK_DEV, D)).reshape(TOKENS, D)
        middle = inputs + attention
        second = low(layer_norm(middle, norm_full[2], norm_full[3]))
        logits = low_back(highest(second, router_full))
        row_max = lax.optimization_barrier(jnp.max(logits, axis=-1, keepdims=True))
        expo = jnp.exp(logits - row_max)
        prob_rows = expo / lax.optimization_barrier(jnp.sum(expo, axis=-1, keepdims=True))
        gate_values = lax.optimization_barrier(jnp.sum(prob_rows[:, None, :] * choose, axis=-1))
        padded = jnp.concatenate([second, jnp.zeros((1, D), jnp.float32)], axis=0)

        def apply_expert(operands):
            slot_source, inner_part, outer_part = operands
            expert_rows = low_back(jnp.take(padded, slot_source, axis=0))
            summed = jnp.zeros((SLOTS, D), jnp.float32)
            for part_index in range(N_HEAD):
                lower = part_index * slice_width
                upper = lower + slice_width
                hidden = highest(low_back(expert_rows), inner_part[:, lower:upper])
                active = low(gelu_tanh(low_back(hidden)))
                summed = summed + low(highest(active, outer_part[lower:upper]))
            return low_back(low(summed))
        outputs = lax.map(jax.checkpoint(apply_expert), (source.reshape(EXPERTS, SLOTS), inner_full, outer_full))
        picked = jnp.take(outputs.reshape(EXPERTS * SLOTS, D), target, axis=0).reshape(TOKENS, 2, D)
        return middle + lax.optimization_barrier(jnp.sum(gate_values[:, :, None] * picked, axis=1))
    inputs = block_input.astype(jnp.float32)
    result, pullback = jax.vjp(forward, inputs, low(qkv_master), low(proj_master), low(router_master), low(norm_master), low(inner_master), low(outer_master))
    gradients = pullback(output_grad.astype(jnp.float32))
    qkv_new = adam_step(qkv_master, qkv_mean, qkv_square, gradients[1], 2.0 * D ** (-0.5))
    proj_new = adam_step(proj_master, proj_mean, proj_square, gradients[2], 2.0 * (D // 16) ** (-0.5))
    router_new = adam_step(router_master, router_mean, router_square, gradients[3], 2.0 * (4 * D) ** (-0.5))
    norm_new = adam_step(norm_master, norm_mean, norm_square, gradients[4], NORM_RATE)
    inner_new = adam_step(inner_master, inner_mean, inner_square, gradients[5], 2.0 * D ** (-0.5))
    outer_new = adam_step(outer_master, outer_mean, outer_square, gradients[6], 2.0 * max(1, FF * 4 // (EXPERTS * EXPERTS)) ** (-0.5))
    return (result.astype(jnp.bfloat16), gradients[0], qkv_new[0], qkv_new[1], qkv_new[2], qkv_new[3], proj_new[0], proj_new[1], proj_new[2], proj_new[3], router_new[0], router_new[1], router_new[2], router_new[3], norm_new[0], norm_new[1], norm_new[2], norm_new[3], inner_new[0], inner_new[1], inner_new[2], inner_new[3], outer_new[0], outer_new[1], outer_new[2], outer_new[3])
```

```python
import functools

import jax
import jax.numpy as jnp
from jax import lax
from jax.experimental import pallas as pl
from jax.experimental.pallas import tpu as pltpu
from jax.sharding import PartitionSpec as P

HD = 64
FF = 3072
SEQ = 197
PAD = 208
STEP = 3

EPS_NORM = 1e-06
BETA_ONE = 0.5
BETA_TWO = 0.5
EPS_ADAM = 1e-08
DECAY = 0.1
NORM_RATE = 0.3

AXES = ("expert", "head")
F32 = jnp.float32
BF16 = jnp.bfloat16
VMEM_BYTES = 60 * 2**20
MESH = pl.DeviceIdType.MESH


def adam_step(master, first_state, square, gradient, step_rate):
    momentum = BETA_ONE * first_state + (1.0 - BETA_ONE) * gradient
    variance = BETA_TWO * square + (1.0 - BETA_TWO) * gradient * gradient
    first_fix = momentum / (1.0 - BETA_ONE**STEP)
    second_fix = variance / (1.0 - BETA_TWO**STEP)
    updated = master - step_rate * (first_fix / (jnp.sqrt(second_fix) + EPS_ADAM) + DECAY * master)
    return (updated, momentum, variance, updated.astype(BF16))


def dot_nn(a, b):
    return lax.dot_general(a, b, (((1,), (0,)), ((), ())), preferred_element_type=F32)


def dot_nt(a, b):
    return lax.dot_general(a, b, (((1,), (1,)), ((), ())), preferred_element_type=F32)


def dot_tn(a, b):
    return lax.dot_general(a, b, (((0,), (0,)), ((), ())), preferred_element_type=F32)


def cost(microseconds):
    return pl.CostEstimate(
        flops=int(microseconds * 1.1e9), bytes_accessed=int(microseconds * 3e6), transcendentals=0
    )


def params(**kw):
    return pltpu.CompilerParams(vmem_limit_bytes=VMEM_BYTES, **kw)


def spot_of(expert_axis, half, part, low):
    quarter = expert_axis // 4
    a, b, c = part // (2 * quarter), (part // quarter) % 2, part % quarter
    return (half * (expert_axis // 2) + a * quarter + c) * 4 + ((a + b + half) % 2) * 2 + low


def row_perm(expert_axis, k):
    return [
        (spot_of(expert_axis, r, f, lo), spot_of(expert_axis, r, f ^ k, lo))
        for r in range(2)
        for lo in range(2)
        for f in range(expert_axis)
    ]


def weight_perm(expert_axis, k):
    return [
        (f * 4 + h, spot_of(expert_axis, (h // 2) ^ k, f, h % 2))
        for f in range(expert_axis)
        for h in range(4)
    ]


def turned(perm):
    return [(b, a) for a, b in perm]


def core_perm(expert_axis):
    return [(d, d ^ 1) for d in range(expert_axis * 4)]


def routing_kernel(ids_ref, wide_ref, tall_ref, wide_out, tall_out, *, experts, cap):
    tokens = wide_ref.shape[1]
    part = ids_ref[0]
    row = lax.broadcasted_iota(jnp.int32, (tokens, tokens), 0)
    col = lax.broadcasted_iota(jnp.int32, (tokens, tokens), 1)

    wide = wide_ref[...] ^ part
    names = lax.broadcasted_iota(jnp.int32, (experts, tokens), 0)
    first, second = wide[0:1, :] == names, wide[1:2, :] == names
    seen = (first | second).astype(F32)
    before = dot_nn(seen.astype(BF16), (row < col).astype(BF16))
    place = jnp.concatenate(
        [
            jnp.sum(jnp.where(first, before, 0.0), axis=0, keepdims=True),
            jnp.sum(jnp.where(second, before, 0.0), axis=0, keepdims=True),
        ],
        axis=0,
    ).astype(jnp.int32)
    wide_out[...] = jnp.where(wide_ref[...] < 0, -1, wide * cap + place)

    tall = tall_ref[...] ^ part
    names = lax.broadcasted_iota(jnp.int32, (tokens, experts), 1)
    first, second = tall[:, 0:1] == names, tall[:, 1:2] == names
    seen = (first | second).astype(F32)
    before = dot_nn((col < row).astype(BF16), seen.astype(BF16))
    place = jnp.concatenate(
        [
            jnp.sum(jnp.where(first, before, 0.0), axis=1, keepdims=True),
            jnp.sum(jnp.where(second, before, 0.0), axis=1, keepdims=True),
        ],
        axis=1,
    ).astype(jnp.int32)
    tall_out[...] = jnp.where(tall_ref[...] < 0, -1, tall * cap + place)


def where_am_i(experts):
    quarter = experts // 4
    at_expert, at_head = lax.axis_index("expert"), lax.axis_index("head")
    half = lax.div(at_expert, experts // 2)
    rest = lax.rem(at_expert, experts // 2)
    a = lax.div(rest, quarter)
    b = lax.rem(lax.div(at_head, 2) + a + half, 2)
    return a * 2 * quarter + b * quarter + lax.rem(rest, quarter), half, lax.rem(at_head, 2)


def flipped(experts, part, k):
    there, bit = jnp.int32(0), 1
    while bit < experts:
        there = there + lax.rem(lax.div(part, bit) + lax.div(jnp.int32(k), bit), 2) * bit
        bit = bit * 2
    return there


def partner(experts, part, half, low, k):
    quarter = experts // 4
    there = flipped(experts, part, k)
    a = lax.div(there, 2 * quarter)
    row = half * (experts // 2) + a * quarter + lax.rem(there, quarter)
    return (row, lax.rem(lax.div(there, quarter) + a + half, 2) * 2 + low)


def block_at(experts, j):
    far = experts // 2
    if isinstance(j, int):
        return far if j == 0 else 0 if j == 1 else j + far - 1 if j <= far else j - far
    return jnp.where(
        j == 0, far, jnp.where(j == 1, 0, jnp.where(j <= far, j + far - 1, j - far))
    )


def greet(devices):
    barrier = pltpu.get_barrier_semaphore()
    for device in devices:
        pl.semaphore_signal(barrier, inc=1, device_id=device, device_id_type=MESH)
    pl.semaphore_wait(barrier, len(devices))


def picked_rows(wide_ref, rows, k, cap):
    slot = lax.broadcasted_iota(jnp.int32, (cap, rows.shape[0]), 0)
    first = wide_ref[0:1, :] - k * cap
    second = wide_ref[1:2, :] - k * cap
    pick = ((first == slot) | (second == slot)).astype(F32).astype(BF16)
    return dot_nn(pick, rows).astype(BF16)


def my_bits(count, index):
    return [lax.rem(lax.div(index, 2 ** (count - 1 - d)), 2) for d in range(count)]


def across(bits, low, d):
    place = jnp.int32(0)
    for i, bit in enumerate(bits):
        place = place * 2 + (1 - bit if i == d else bit)
    place = place * 2 + low
    return (lax.div(place, 4), lax.rem(place, 4))


def region(bits, full, d=None, flipped=False):
    return tuple(
        slice(None) if i in full else (1 - bit if (flipped and i == d) else bit)
        for i, bit in enumerate(bits)
    )


def parts_of(half_width):
    tiles = half_width // 128
    first = -(-tiles // 2) * 128
    return (slice(0, first), slice(first, half_width))


def gather_kernel(
    own_ref,
    wall_ref,
    twin,
    wall,
    twin_sem,
    step_send,
    step_recv,
    pass_send,
    pass_recv,
    own_sem,
):
    at_expert, at_head = lax.axis_index("expert"), lax.axis_index("head")
    low = lax.rem(at_head, 2)
    count = wall.ndim - 3
    bits = my_bits(count, lax.div(at_expert * 4 + at_head, 2))
    sibling = (at_expert, at_head + 1 - 2 * low)
    greet([sibling] + [across(bits, low, d) for d in range(count)])
    twin_copy = pltpu.make_async_remote_copy(
        src_ref=own_ref,
        dst_ref=twin,
        send_sem=twin_sem.at[0],
        recv_sem=twin_sem.at[1],
        device_id=sibling,
        device_id_type=MESH,
    )
    twin_copy.start()
    own_rows = own_ref.shape[0]
    half_width = wall.shape[-1]
    mine = tuple(bits)
    cols = parts_of(half_width)
    orders = (list(range(count)), list(range(count - 2)) + [count - 1, count - 2])

    def step_copy(q, i):
        full, d = set(orders[q][:i]), orders[q][i]
        at = (low,) + region(bits, full) + (slice(None), cols[q])
        return pltpu.make_async_remote_copy(
            src_ref=wall.at[at],
            dst_ref=wall.at[at],
            send_sem=step_send.at[q, i],
            recv_sem=step_recv.at[q, i],
            device_id=across(bits, low, d),
            device_id_type=MESH,
        )

    def pass_copy(q, i):
        full, d = set(orders[q][:i]), orders[q][i]
        at = (low,) + region(bits, full, d, True) + (slice(None), cols[q])
        return pltpu.make_async_remote_copy(
            src_ref=wall.at[at],
            dst_ref=wall.at[at],
            send_sem=pass_send.at[q, i],
            recv_sem=pass_recv.at[q, i],
            device_id=sibling,
            device_id_type=MESH,
        )

    twin_copy.wait()
    first = low == 0
    for side in range(2):
        at = slice(side * half_width, (side + 1) * half_width)
        ours, theirs = own_ref[:, at], twin[:, at]
        wall[(side,) + mine] = jnp.concatenate(
            [jnp.where(first, ours, theirs), jnp.where(first, theirs, ours)], axis=0
        ).astype(BF16)
    for i in range(count):
        for q in range(2):
            if i:
                step_copy(q, i - 1).wait_recv()
            step_copy(q, i).start()
        for q in range(2):
            if i:
                pass_copy(q, i - 1).start()
    for q in range(2):
        step_copy(q, count - 1).wait_recv()
        pass_copy(q, count - 1).start()
    for i in range(count):
        for q in range(2):
            step_copy(q, i).wait_send()
            pass_copy(q, i).wait()
    wall_copy = pltpu.make_async_copy(wall, wall_ref, own_sem)
    wall_copy.start()
    wall_copy.wait()


def reduce_kernel(
    all_ref,
    out_ref,
    total,
    landed,
    last,
    spare,
    pair_sem,
    step_send,
    step_recv,
    last_sem,
    *landings,
):
    at_expert, at_head = lax.axis_index("expert"), lax.axis_index("head")
    low = lax.rem(at_head, 2)
    count = all_ref.ndim - 3
    bits = my_bits(count, lax.div(at_expert * 4 + at_head, 2))
    sibling = (at_expert, at_head + 1 - 2 * low)
    greet([sibling] + [across(bits, low, d) for d in range(count)])
    half_width = all_ref.shape[-1]
    cols = parts_of(half_width)
    backwards = list(range(count))[::-1]
    orders = (backwards, [backwards[1], backwards[0]] + backwards[2:])

    def pair_copy(q):
        at = (slice(None),) * count + (slice(None), cols[q])
        return pltpu.make_async_remote_copy(
            src_ref=all_ref.at[(1 - low,) + at],
            dst_ref=landed.at[at],
            send_sem=pair_sem.at[q],
            recv_sem=pair_sem.at[2 + q],
            device_id=sibling,
            device_id_type=MESH,
        )

    def step_copy(q, i):
        gone, d = orders[q][:i], orders[q][i]
        full = set(range(count)) - set(gone) - {d}
        at = region(bits, full, d, True) + (slice(None), cols[q])
        return pltpu.make_async_remote_copy(
            src_ref=total.at[at],
            dst_ref=landings[q * count + i],
            send_sem=step_send.at[q, i],
            recv_sem=step_recv.at[q, i],
            device_id=across(bits, low, d),
            device_id_type=MESH,
        )

    for q in range(2):
        pair_copy(q).start()
    for q in range(2):
        at = (slice(None),) * count + (slice(None), cols[q])
        pair_copy(q).wait_recv()
        total[at] = (all_ref[(low,) + at].astype(F32) + landed[at].astype(F32)).astype(BF16)
        step_copy(q, 0).start()
    for i in range(count):
        for q in range(2):
            step_copy(q, i).wait_recv()
            gone, d = orders[q][:i], orders[q][i]
            full = set(range(count)) - set(gone) - {d}
            at = region(bits, full) + (slice(None), cols[q])
            added = total[at].astype(F32) + landings[q * count + i][...].astype(F32)
            if i < count - 1:
                total[at] = added.astype(BF16)
                step_copy(q, i + 1).start()
            else:
                last[:, cols[q]] = added
    own_rows = out_ref.shape[0]
    top, bottom = last[0:own_rows, :], last[own_rows:, :]
    first = low == 0
    spare[0] = jnp.where(first, bottom, top)
    last_copy = pltpu.make_async_remote_copy(
        src_ref=spare.at[0],
        dst_ref=spare.at[1],
        send_sem=last_sem.at[0],
        recv_sem=last_sem.at[1],
        device_id=sibling,
        device_id_type=MESH,
    )
    last_copy.start()
    ours = jnp.where(first, top, bottom)
    last_copy.wait()
    theirs = spare[1]
    out_ref[:, 0:half_width] = jnp.where(first, ours, theirs)
    out_ref[:, half_width:] = jnp.where(first, theirs, ours)
    for q in range(2):
        pair_copy(q).wait_send()
        for i in range(count):
            step_copy(q, i).wait_send()


def norm_parts(values):
    centered = values - jnp.mean(values, axis=-1, keepdims=True)
    spread = lax.rsqrt(jnp.mean(centered * centered, axis=-1, keepdims=True) + EPS_NORM)
    return centered * spread, spread


def norm_back(grad, unit, spread, gain):
    scaled = grad * gain
    return spread * (
        scaled
        - jnp.mean(scaled, axis=-1, keepdims=True)
        - unit * jnp.mean(scaled * unit, axis=-1, keepdims=True)
    )


def forward_kernel(
    x_ref,
    wall_ref,
    wide_ref,
    gy_ref,
    qkv_ref,
    o_ref,
    h_ref,
    n2_ref,
    p_ref,
    out_ref,
    small,
    held,
    send_sem,
    recv_sem,
    own_sem,
    *,
    experts,
    cap,
):
    width = x_ref.shape[2]
    part, half, low = where_am_i(experts)

    def swap_copy(k):
        return pltpu.make_async_remote_copy(
            src_ref=held.at[k],
            dst_ref=out_ref.at[k],
            send_sem=send_sem.at[k],
            recv_sem=recv_sem.at[k],
            device_id=partner(experts, part, half, low, k),
            device_id_type=MESH,
        )

    own_copy = pltpu.make_async_copy(held.at[0], out_ref.at[0], own_sem)

    @pl.when(pl.program_id(0) == 0)
    def _():
        greet([partner(experts, part, half, low, k) for k in range(1, experts)])
        rows = gy_ref[...]
        for k in range(experts - 1, 0, -1):
            held[k] = picked_rows(wide_ref, rows, k, cap)
            swap_copy(k).start()
        held[0] = picked_rows(wide_ref, rows, 0, cap)
        own_copy.start()
        small[...] = wall_ref[0, :, 2 * width :].astype(F32).T

    x = x_ref[0].astype(F32)
    gain, shift = small[experts : experts + 1, :], small[experts + 1 : experts + 2, :]
    unit, _ = norm_parts(x)
    n1 = (unit * gain + shift).astype(BF16)
    for j in range(3):
        qkv_ref[0, :, j * width : (j + 1) * width] = dot_nn(
            n1, wall_ref[j // 2, :, (j % 2) * width : (j % 2 + 1) * width]
        ).astype(BF16)
    lane = lax.broadcasted_iota(jnp.int32, (PAD, 128), 1)
    key_at = lax.broadcasted_iota(jnp.int32, (PAD, PAD), 1)
    for pair in range(width // 128):
        q = qkv_ref[0, :, pair * 128 : (pair + 1) * 128]
        k = qkv_ref[0, :, width + pair * 128 : width + (pair + 1) * 128]
        v = qkv_ref[0, :, 2 * width + pair * 128 : 2 * width + (pair + 1) * 128]
        halves = []
        for side in range(2):
            mine = (lane < HD) if side == 0 else (lane >= HD)
            scores = dot_nt(jnp.where(mine, q, jnp.zeros_like(q)), k) * (HD**-0.5)
            scores = jnp.where(key_at < SEQ, scores, -1e30)
            expo = jnp.exp(scores - jnp.max(scores, axis=-1, keepdims=True))
            probs = expo / jnp.sum(expo, axis=-1, keepdims=True)
            halves.append(dot_nn(probs.astype(BF16), v))
        o_ref[0, :, pair * 128 : (pair + 1) * 128] = jnp.where(
            lane < HD, halves[0], halves[1]
        ).astype(BF16)
    h = x + dot_nn(o_ref[0], wall_ref[1, :, width : 2 * width])
    h_ref[0] = h
    gain, shift = small[experts + 2 : experts + 3, :], small[experts + 3 : experts + 4, :]
    unit, _ = norm_parts(h)
    n2 = (unit * gain + shift).astype(BF16)
    n2_ref[0] = n2
    logits = dot_nt(small[0:experts, :].astype(BF16), n2)
    expo = jnp.exp(logits - jnp.max(logits, axis=0, keepdims=True))
    p_ref[0] = expo / jnp.sum(expo, axis=0, keepdims=True)

    @pl.when(pl.program_id(0) == pl.num_programs(0) - 1)
    def _():
        for k in range(1, experts):
            swap_copy(k).wait()
        own_copy.wait()


def expert_kernel(
    wide_ref,
    rows_ref,
    g_ref,
    w0_ref,
    w1_ref,
    w2_ref,
    w3_ref,
    router_ref,
    y_ref,
    dr_ref,
    in0_ref,
    out0_ref,
    in1_ref,
    out1_ref,
    x_all,
    g_all,
    held,
    w_all,
    acc,
    y_acc,
    dr_acc,
    x_send,
    x_recv,
    y_sem,
    dr_send,
    dr_recv,
    g_sem,
    w_sem,
    own_sem,
    pair_sem,
    ready_sem,
    *,
    experts,
    cap,
    group,
):
    part, half, low = where_am_i(experts)
    at_expert, at_head = lax.axis_index("expert"), lax.axis_index("head")
    sibling = (at_expert, at_head + 1 - 2 * low)
    greet([partner(experts, part, half, low, k) for k in range(1, experts)] + [sibling])
    sequence = [block_at(experts, j) for j in range(experts)]
    width = x_all.shape[2]
    slice_width = w_all.shape[2]
    tile = group * cap

    def x_copy(k):
        return pltpu.make_async_remote_copy(
            src_ref=held.at[k],
            dst_ref=x_all.at[k, pl.ds(0, cap), :],
            send_sem=x_send.at[k],
            recv_sem=x_recv.at[k],
            device_id=partner(experts, part, half, low, k),
            device_id_type=MESH,
        )

    def y_copy(k):
        return pltpu.make_async_copy(g_all.at[k], y_ref.at[k], y_sem.at[k])

    def dr_copy(k):
        return pltpu.make_async_remote_copy(
            src_ref=x_all.at[k],
            dst_ref=dr_ref.at[k],
            send_sem=dr_send.at[k],
            recv_sem=dr_recv.at[k],
            device_id=partner(experts, part, half, low, k),
            device_id_type=MESH,
        )

    weights = [
        pltpu.make_async_copy(w, w_all.at[j], w_sem.at[j])
        for j, w in enumerate((w0_ref, w1_ref, w2_ref, w3_ref))
    ]
    for copy in weights:
        copy.start()
    g_copy = pltpu.make_async_copy(g_ref, g_all, g_sem)
    g_copy.start()
    rows = rows_ref[...]
    for k in sequence:
        if k:
            held[k] = picked_rows(wide_ref, rows, k, cap)
            x_copy(k).start()
    x_all[0, 0:cap, :] = picked_rows(wide_ref, rows, 0, cap)
    acc[...] = jnp.zeros_like(acc)
    g_copy.wait()
    for copy in weights:
        copy.wait()

    def one_tile(t, _):
        base = t * group
        names = [block_at(experts, base + j) for j in range(group)]
        for k in names:

            @pl.when(k > 0)
            def _(k=k):
                x_copy(k).wait_recv()

        x = jnp.concatenate([x_all[k, 0:cap, :] for k in names], axis=0)
        g = jnp.concatenate([g_all[k] for k in names], axis=0)
        logits = dot_nt(x, router_ref[...])
        expo = jnp.exp(logits - jnp.max(logits, axis=-1, keepdims=True))
        probs = expo / jnp.sum(expo, axis=-1, keepdims=True)
        name = lax.broadcasted_iota(jnp.int32, probs.shape, 1)
        gate = jnp.sum(jnp.where(name == part, probs, 0.0), axis=-1, keepdims=True)
        dy = (gate * g.astype(F32)).astype(BF16)
        x_turned, dy_turned = x.T, dy.T

        def first(s):
            w_in = w_all[s, 0:width, :]
            w_out = w_all[s, width : 2 * width, :]
            acts, dus = [], []
            for i in range(0, slice_width, 256):
                u = dot_nn(x, w_in[:, i : i + 256])
                da = dot_nt(dy, w_out[i : i + 256, :])
                root = 0.7978845608028654
                sq = u * u
                th = jnp.tanh(u * (root + (root * 0.044715) * sq))
                plus = 0.5 + 0.5 * th
                acts.append((u * plus).astype(BF16))
                slope = plus + (0.5 * u) * (1.0 - th * th) * (root + (3.0 * root * 0.044715) * sq)
                dus.append((da * slope).astype(BF16))
            return jnp.concatenate(acts, axis=1), jnp.concatenate(dus, axis=1), w_in, w_out

        def second(s, fresh, act, du, w_in, w_out):
            y_part, dr_part = dot_nn(act, w_out), dot_nt(du, w_in)
            y_acc[...] = y_part if fresh else y_acc[...] + y_part
            dr_acc[...] = dr_part if fresh else dr_acc[...] + dr_part
            acc[s, 0] += dot_nn(x_turned, du)
            acc[s, 1] += dot_nn(dy_turned, act)

        order = (2, 3, 0, 1)
        kept = first(order[0])
        for i in range(1, 4):
            fresh = first(order[i])
            second(order[i - 1], i == 1, *kept)
            kept = fresh
        second(order[3], False, *kept)

        y = y_acc[...]
        dgate = jnp.sum(g.astype(F32) * y, axis=-1, keepdims=True)
        dr_low, y_low = dr_acc[...].astype(BF16), (gate * y).astype(BF16)
        for j, k in enumerate(names):
            x_all[k, 0:cap, :] = dr_low[j * cap : (j + 1) * cap, :]
            g_all[k] = y_low[j * cap : (j + 1) * cap, :]
            line = jnp.broadcast_to(dgate[j * cap : (j + 1) * cap, :], (cap, 128))
            if cap % 128:
                line = jnp.concatenate([line, jnp.zeros((128 - cap % 128, 128), F32)], axis=0)
            line = line.T[0:1, :]
            top = line.astype(BF16).astype(F32)
            middle = (line - top).astype(BF16).astype(F32)
            last = line - top - middle
            long = line.shape[1]
            meta = jnp.concatenate([top, middle, last, jnp.zeros((13, long), F32)], axis=0)
            meta = jnp.concatenate([meta, jnp.zeros((16, width - long), F32)], axis=1)
            x_all[k, cap : cap + 16, :] = meta.astype(BF16)

        for k in names:

            @pl.when(k > 0)
            def _(k=k):
                dr_copy(k).start()

            @pl.when(k == 0)
            def _():
                pltpu.make_async_copy(x_all.at[0], dr_ref.at[0], own_sem).start()

            y_copy(k).start()

        return 0

    lax.fori_loop(0, experts // group, one_tile, 0)

    pl.semaphore_signal(ready_sem, inc=1, device_id=sibling, device_id_type=MESH)
    for j in range(2):
        for side in range(2):
            w_all[j, side * width : (side + 1) * width, :] = acc[2 + j, side].astype(BF16)
    pl.semaphore_wait(ready_sem, 1)
    swaps = [
        pltpu.make_async_remote_copy(
            src_ref=w_all.at[j],
            dst_ref=w_all.at[2 + j],
            send_sem=pair_sem.at[j],
            recv_sem=pair_sem.at[2 + j],
            device_id=sibling,
            device_id_type=MESH,
        )
        for j in range(2)
    ]
    for copy in swaps:
        copy.start()
    results = []
    for j in range(2):
        swaps[j].wait()
        for side in range(2):
            at = slice(side * width, (side + 1) * width)
            w_all[2 + j, at, :] = (w_all[2 + j, at, :].astype(F32) + acc[j, side]).astype(BF16)
        for side, ref in enumerate(((in0_ref, out0_ref), (in1_ref, out1_ref))[j]):
            at = pl.ds(side * width, width)
            results.append(
                pltpu.make_async_copy(w_all.at[2 + j, at, :], ref, w_sem.at[2 * j + side])
            )
            results[-1].start()
    for copy in results:
        copy.wait()

    def settle(k, _):
        x_copy(k).wait_send()
        dr_copy(k).wait()
        y_copy(k).wait()
        return 0

    lax.fori_loop(1, experts, settle, 0)
    y_copy(0).wait()
    pltpu.make_async_copy(x_all.at[0], dr_ref.at[0], own_sem).wait()


def backward_kernel(
    tall_ref,
    gy_ref,
    x_ref,
    h_ref,
    qkv_ref,
    o_ref,
    p_ref,
    wall_ref,
    dr_ref,
    y_ref,
    grad_ref,
    all_ref,
    out_ref,
    small,
    acc,
    small_acc,
    dqkv,
    dp_all,
    y_in,
    send_sem,
    recv_sem,
    own_sem,
    *,
    experts,
    cap,
):
    width = x_ref.shape[2]
    part, half, low = where_am_i(experts)
    step = pl.program_id(0)

    def swap_copy(k):
        return pltpu.make_async_remote_copy(
            src_ref=y_ref.at[k],
            dst_ref=y_in.at[k],
            send_sem=send_sem.at[k],
            recv_sem=recv_sem.at[k],
            device_id=partner(experts, part, half, low, k),
            device_id_type=MESH,
        )

    own_copy = pltpu.make_async_copy(y_ref.at[0], y_in.at[0], own_sem)

    @pl.when(step == 0)
    def _():
        greet([partner(experts, part, half, low, k) for k in range(1, experts)])
        for k in range(experts - 1, 0, -1):
            swap_copy(k).start()
        own_copy.start()
        small[...] = wall_ref[0, :, 2 * width :].astype(F32).T
        acc[...] = jnp.zeros_like(acc)
        small_acc[...] = jnp.zeros_like(small_acc)

    gy = gy_ref[0].astype(F32)
    h = h_ref[step]
    unit, spread = norm_parts(h)
    gain, shift = small[experts + 2 : experts + 3, :], small[experts + 3 : experts + 4, :]
    n2 = (unit * gain + shift).astype(BF16)
    slot = lax.broadcasted_iota(jnp.int32, (PAD, cap), 1)

    def owners(image, k):
        first = tall_ref[image, :, 0:1] - k * cap
        second = tall_ref[image, :, 1:2] - k * cap
        return ((first == slot) | (second == slot)).astype(F32).astype(BF16)

    dn2 = jnp.zeros((PAD, width), F32)
    for k in range(experts):
        pick = owners(step, k)
        dn2 = dn2 + dot_nn(pick, dr_ref[k, 0:cap, :])
        line = dot_nt(dr_ref[k, cap : cap + 16, 0:cap], pick)
        dp_all[pl.ds(flipped(experts, part, k), 1), :] = (
            line[0:1, :] + line[1:2, :] + line[2:3, :]
        )
    probs = p_ref[0]
    dp = dp_all[...]
    dlogits = (probs * (dp - jnp.sum(dp * probs, axis=0, keepdims=True))).astype(BF16)
    small_acc[0:experts, :] += dot_nn(dlogits, n2)
    dn2 = dn2 + dot_tn(dlogits, small[0:experts, :].astype(BF16))
    small_acc[experts + 2 : experts + 3, :] += jnp.sum(dn2 * unit, axis=0, keepdims=True)
    small_acc[experts + 3 : experts + 4, :] += jnp.sum(dn2, axis=0, keepdims=True)
    dh = gy + norm_back(dn2, unit, spread, gain)
    dh_low = dh.astype(BF16)
    acc[:, 3 * width :] += dot_tn(o_ref[0], dh_low)
    do = dot_nt(dh_low, wall_ref[1, :, width : 2 * width]).astype(BF16)

    lane = lax.broadcasted_iota(jnp.int32, (PAD, 128), 1)
    key_at = lax.broadcasted_iota(jnp.int32, (PAD, PAD), 0)
    for pair in range(width // 128):
        q = qkv_ref[0, :, pair * 128 : (pair + 1) * 128]
        k = qkv_ref[0, :, width + pair * 128 : width + (pair + 1) * 128]
        v = qkv_ref[0, :, 2 * width + pair * 128 : 2 * width + (pair + 1) * 128]
        dop = do[:, pair * 128 : (pair + 1) * 128]
        parts = []
        for side in range(2):
            mine = (lane < HD) if side == 0 else (lane >= HD)
            k_mine = jnp.where(mine, k, jnp.zeros_like(k))
            v_mine = jnp.where(mine, v, jnp.zeros_like(v))
            scores = dot_nt(k_mine, q) * (HD**-0.5)
            scores = jnp.where(key_at < SEQ, scores, -1e30)
            expo = jnp.exp(scores - jnp.max(scores, axis=0, keepdims=True))
            prob = expo / jnp.sum(expo, axis=0, keepdims=True)
            dprob = dot_nt(v_mine, dop)
            dscore = prob * (dprob - jnp.sum(dprob * prob, axis=0, keepdims=True))
            dz = (dscore * (HD**-0.5)).astype(BF16)
            parts.append((dot_tn(dz, k), dot_nn(dz, q), dot_nn(prob.astype(BF16), dop)))
        for j in range(3):
            dqkv[:, j * width + pair * 128 : j * width + (pair + 1) * 128] = jnp.where(
                lane < HD, parts[0][j], parts[1][j]
            ).astype(BF16)

    unit, spread = norm_parts(x_ref[0].astype(F32))
    gain, shift = small[experts : experts + 1, :], small[experts + 1 : experts + 2, :]
    n1 = (unit * gain + shift).astype(BF16)
    dn1 = jnp.zeros((PAD, width), F32)
    for j in range(3):
        cols = slice(j * width, (j + 1) * width)
        acc[:, cols] += dot_tn(n1, dqkv[:, cols])
        dn1 = dn1 + dot_nt(
            dqkv[:, cols], wall_ref[j // 2, :, (j % 2) * width : (j % 2 + 1) * width]
        )
    small_acc[experts : experts + 1, :] += jnp.sum(dn1 * unit, axis=0, keepdims=True)
    small_acc[experts + 1 : experts + 2, :] += jnp.sum(dn1, axis=0, keepdims=True)
    grad_ref[0] = dh + norm_back(dn1, unit, spread, gain)

    @pl.when(step == pl.num_programs(0) - 1)
    def _():
        for j in range(4):
            all_ref[j // 2, :, (j % 2) * width : (j % 2 + 1) * width] = acc[
                :, j * width : (j + 1) * width
            ].astype(BF16)
        all_ref[0, :, 2 * width :] = small_acc[...].T.astype(BF16)
        all_ref[1, :, 2 * width :] = jnp.zeros((width, 128), BF16)
        for k in range(1, experts):
            swap_copy(k).wait()
        own_copy.wait()

        def one_image(image, _):
            total = h_ref[image]
            for k in range(experts):
                total = total + dot_nn(owners(image, k), y_in[k])
            out_ref[image] = total.astype(BF16)
            return 0

        lax.fori_loop(0, out_ref.shape[0], one_image, 0)


def adam_kernel(m_ref, f_ref, q_ref, a_ref, b_ref, w_out, f_out, q_out, c_out, *, rate, turn):
    grad = a_ref[...].astype(F32) + b_ref[...].astype(F32)
    if turn:
        grad = grad.T
    new = adam_step(m_ref[...], f_ref[...], q_ref[...], grad, rate)
    w_out[...], f_out[...], q_out[...], c_out[...] = new


def expert_adam(master, first_state, square, grads, rate, turn):
    shape = master.shape
    rows, cols = shape[1], shape[2]
    block = 128
    here = pl.BlockSpec((block, cols), lambda i: (i, 0))
    there = pl.BlockSpec((cols, block), lambda i: (0, i)) if turn else here
    new = pl.pallas_call(
        functools.partial(adam_kernel, rate=rate, turn=turn),
        grid=(rows // block,),
        out_shape=[jax.ShapeDtypeStruct((rows, cols), t) for t in (F32, F32, F32, BF16)],
        in_specs=[here, here, here, there, there],
        out_specs=[here] * 4,
        compiler_params=params(),
        cost_estimate=cost(9),
        name="adam",
    )(*(v.reshape(rows, cols) for v in (master, first_state, square)), *grads)
    return tuple(v.reshape(shape) for v in new)


def on_device(
    expert_axis,
    block_input,
    output_grad,
    routes,
    qkv_master,
    qkv_mean,
    qkv_square,
    proj_master,
    proj_mean,
    proj_square,
    router_master,
    router_mean,
    router_square,
    norm_master,
    norm_mean,
    norm_square,
    inner_master,
    inner_mean,
    inner_square,
    outer_master,
    outer_mean,
    outer_square,
):
    row_count, width = block_input.shape
    heads = width // HD
    images = row_count // SEQ
    tokens = images * PAD
    experts = router_master.shape[1]
    own_rows = qkv_master.shape[0]
    bound = row_count * 16 // (5 * experts) + 1
    cap = -(-bound // 16) * 16
    group = max(1, min(experts, 640 // cap // 2 * 2))
    while experts % group:
        group = group - 1
    slice_width = inner_master.shape[2]
    vmem = pl.BlockSpec(memory_space=pltpu.VMEM)
    smem = pl.BlockSpec(memory_space=pltpu.SMEM)
    anywhere = pl.BlockSpec(memory_space=pl.ANY)
    struct = jax.ShapeDtypeStruct

    ids = where_am_i(experts)[0].reshape(1).astype(jnp.int32)

    qkv_own = qkv_master.reshape(own_rows, heads, 3, HD).transpose(0, 2, 1, 3)
    qkv_own = qkv_own.reshape(own_rows, 3 * width)
    wall_own = jnp.concatenate(
        [
            qkv_own[:, : 2 * width],
            router_master,
            norm_master.T,
            jnp.zeros((own_rows, 128 - experts - 4), F32),
            qkv_own[:, 2 * width :],
            proj_master,
            jnp.zeros((own_rows, 128), F32),
        ],
        axis=1,
    )
    half_width = 2 * width + 128
    count = (width // own_rows).bit_length() - 2
    block = (2,) * count + (2 * own_rows, half_width)
    in_kernel = own_rows % 8 == 0

    both = jnp.concatenate([inner_master[0].astype(BF16), outer_master[0].astype(BF16)], axis=0)
    w_own = [lax.ppermute(both, AXES, weight_perm(experts, k)) for k in range(2)]

    def padded(values):
        return jnp.pad(values.reshape(images, SEQ, -1), ((0, 0), (0, PAD - SEQ), (0, 0)))

    tall = jnp.pad(
        routes.reshape(images, SEQ, 2), ((0, 0), (0, PAD - SEQ), (0, 0)), constant_values=-1
    ).reshape(tokens, 2)
    wide_slots, tall_slots = pl.pallas_call(
        functools.partial(routing_kernel, experts=experts, cap=cap),
        out_shape=(struct((2, tokens), jnp.int32), struct((tokens, 2), jnp.int32)),
        in_specs=[smem, vmem, vmem],
        out_specs=(vmem, vmem),
        compiler_params=params(),
        name="routing",
    )(ids, tall.T, tall)
    tall_slots = tall_slots.reshape(images, PAD, 2)

    gy = padded(output_grad)
    dma = pltpu.SemaphoreType.DMA
    wall = pl.pallas_call(
        gather_kernel,
        out_shape=struct((2,) + block, BF16),
        in_specs=[vmem],
        out_specs=anywhere,
        scratch_shapes=[
            pltpu.VMEM(wall_own.shape, F32),
            pltpu.VMEM((2,) + block, BF16),
            dma((2,)),
        ]
        + [dma((2, count))] * 4
        + [dma],
        compiler_params=params(collective_id=0, has_side_effects=True),
        cost_estimate=cost(50),
        name="gather_shared",
    )(wall_own)
    wall = wall.reshape(2, width, half_width)

    x = padded(block_input)

    def image_spec(*dims):
        return pl.BlockSpec((1,) + dims, lambda i: (i,) + (0,) * len(dims))

    def whole_spec(*dims, once=True):
        mode = dict(pipeline_mode=pl.Buffered(1)) if once else {}
        return pl.BlockSpec(dims, lambda i: (0,) * len(dims), **mode)

    qkv, attended, middle, second, probs, g_blocks = pl.pallas_call(
        functools.partial(forward_kernel, experts=experts, cap=cap),
        grid=(images,),
        out_shape=(
            struct((images, PAD, 3 * width), BF16),
            struct((images, PAD, width), BF16),
            struct((images, PAD, width), F32),
            struct((images, PAD, width), BF16),
            struct((images, experts, PAD), F32),
            struct((experts, cap, width), BF16),
        ),
        in_specs=[
            image_spec(PAD, width),
            whole_spec(2, width, half_width),
            whole_spec(2, tokens),
            whole_spec(tokens, width),
        ],
        out_specs=(
            image_spec(PAD, 3 * width),
            image_spec(PAD, width),
            image_spec(PAD, width),
            image_spec(PAD, width),
            image_spec(experts, PAD),
            anywhere,
        ),
        scratch_shapes=[
            pltpu.VMEM((128, width), F32),
            pltpu.VMEM((experts, cap, width), BF16),
            dma((experts,)),
            dma((experts,)),
            dma,
        ],
        compiler_params=params(collective_id=3, has_side_effects=True),
        cost_estimate=cost(50),
        name="forward",
    )(x, wall, wide_slots, gy.reshape(tokens, width))

    w_own_late, second = lax.optimization_barrier((w_own, second))
    w_sib = [lax.ppermute(w, AXES, core_perm(experts)) for w in w_own_late]
    router_low = wall[0, :, 2 * width : 2 * width + experts].T
    y_blocks, dr_blocks, in0, out0, in1, out1 = pl.pallas_call(
        functools.partial(expert_kernel, experts=experts, cap=cap, group=group),
        out_shape=(
            struct((experts, cap, width), BF16),
            struct((experts, cap + 16, width), BF16),
        )
        + (struct((width, slice_width), BF16),) * 4,
        in_specs=[vmem, vmem] + [anywhere] * 5 + [vmem],
        out_specs=[anywhere] * 6,
        scratch_shapes=[
            pltpu.VMEM((experts, cap + 16, width), BF16),
            pltpu.VMEM((experts, cap, width), BF16),
            pltpu.VMEM((experts, cap, width), BF16),
            pltpu.VMEM((4, 2 * width, slice_width), BF16),
            pltpu.VMEM((4, 2, width, slice_width), F32),
            pltpu.VMEM((group * cap, width), F32),
            pltpu.VMEM((group * cap, width), F32),
        ]
        + [dma((experts,))] * 5
        + [dma, dma((4,)), dma, dma((4,)), pltpu.SemaphoreType.REGULAR],
        compiler_params=params(collective_id=1, has_side_effects=True),
        cost_estimate=cost(140),
        name="experts",
    )(wide_slots, second.reshape(tokens, width), g_blocks, *w_own_late, *w_sib, router_low)

    grad_back = [
        [lax.ppermute(g, AXES, turned(weight_perm(experts, k))) for k, g in enumerate(pair)]
        for pair in ((in0, in1), (out0, out1))
    ]

    input_grad, shared_grad, block_output = pl.pallas_call(
        functools.partial(backward_kernel, experts=experts, cap=cap),
        grid=(images,),
        out_shape=(
            struct((images, PAD, width), F32),
            struct((2, width, half_width), BF16),
            struct((images, PAD, width), BF16),
        ),
        in_specs=[
            whole_spec(images, PAD, 2),
            image_spec(PAD, width),
            image_spec(PAD, width),
            whole_spec(images, PAD, width),
            image_spec(PAD, 3 * width),
            image_spec(PAD, width),
            image_spec(experts, PAD),
            whole_spec(2, width, half_width),
            whole_spec(experts, cap + 16, width),
            anywhere,
        ],
        out_specs=(
            image_spec(PAD, width),
            whole_spec(2, width, half_width, once=False),
            whole_spec(images, PAD, width, once=False),
        ),
        scratch_shapes=[
            pltpu.VMEM((128, width), F32),
            pltpu.VMEM((width, 4 * width), F32),
            pltpu.VMEM((128, width), F32),
            pltpu.VMEM((PAD, 3 * width), BF16),
            pltpu.VMEM((experts, PAD), F32),
            pltpu.VMEM((experts, cap, width), BF16),
            dma((experts,)),
            dma((experts,)),
            dma,
        ],
        compiler_params=params(collective_id=4, has_side_effects=True),
        cost_estimate=cost(60),
        name="backward",
    )(tall_slots, gy, x, middle, qkv, attended, probs, wall, dr_blocks, y_blocks)
    input_grad = input_grad[:, :SEQ].reshape(row_count, width)
    block_output = block_output[:, :SEQ].reshape(row_count, width)

    landings = [
        pltpu.VMEM((2,) * (count - 1 - i) + (2 * own_rows, c.stop - c.start), BF16)
        for c in parts_of(half_width)
        for i in range(count)
    ]
    shared_own = pl.pallas_call(
        reduce_kernel,
        out_shape=struct((own_rows, 2 * half_width), F32),
        in_specs=[vmem],
        out_specs=vmem,
        scratch_shapes=[
            pltpu.VMEM(block, BF16),
            pltpu.VMEM(block, BF16),
            pltpu.VMEM((2 * own_rows, half_width), F32),
            pltpu.VMEM((2, own_rows, half_width), F32),
            dma((4,)),
            dma((2, count)),
            dma((2, count)),
            dma((2,)),
        ]
        + landings,
        compiler_params=params(collective_id=2, has_side_effects=True),
        cost_estimate=cost(50),
        name="reduce_shared",
    )(shared_grad.reshape((2,) + block))
    qkv_owned = jnp.concatenate(
        [shared_own[:, : 2 * width], shared_own[:, half_width : half_width + width]], axis=1
    )
    qkv_owned = qkv_owned.reshape(own_rows, 3, heads, HD).transpose(0, 2, 1, 3)
    qkv_owned = qkv_owned.reshape(own_rows, 3 * width)
    proj_owned = shared_own[:, half_width + width : half_width + 2 * width]
    router_owned = shared_own[:, 2 * width : 2 * width + experts]
    norm_owned = shared_own[:, 2 * width + experts : 2 * width + experts + 4].T

    qkv_new = adam_step(qkv_master, qkv_mean, qkv_square, qkv_owned, 2.0 * width ** (-0.5))
    proj_new = adam_step(
        proj_master, proj_mean, proj_square, proj_owned, 2.0 * (width // 16) ** (-0.5)
    )
    router_new = adam_step(
        router_master, router_mean, router_square, router_owned, 2.0 * (4 * width) ** (-0.5)
    )
    norm_new = adam_step(norm_master, norm_mean, norm_square, norm_owned, NORM_RATE)
    inner_new = expert_adam(
        inner_master, inner_mean, inner_square, grad_back[0], 2.0 * width ** (-0.5), False
    )
    outer_new = expert_adam(
        outer_master,
        outer_mean,
        outer_square,
        grad_back[1],
        2.0 * max(1, FF * 4 // (experts * experts)) ** (-0.5),
        True,
    )
    return (
        block_output,
        input_grad,
        *qkv_new,
        *proj_new,
        *router_new,
        *norm_new,
        *inner_new,
        *outer_new,
    )


def solution(mesh):
    rows = P(AXES, None)
    cols = P(None, AXES)
    inner = P("expert", None, "head")
    outer = P("expert", "head", None)
    in_specs = (rows,) * 12 + (cols,) * 3 + (inner,) * 3 + (outer,) * 3
    out_specs = (rows,) * 14 + (cols,) * 4 + (inner,) * 4 + (outer,) * 4
    return jax.shard_map(
        functools.partial(on_device, mesh.shape["expert"]),
        mesh=mesh,
        in_specs=in_specs,
        out_specs=out_specs,
        check_vma=False,
    )
```

```python
import functools

import jax
import jax.numpy as jnp
from jax import lax
from jax.experimental import pallas as pl
from jax.experimental.pallas import tpu as pltpu
from jax.sharding import PartitionSpec as P

HD = 64
FF = 3072
SEQ = 197
PAD = 208
STEP = 3

EPS_NORM = 1e-06
BETA_ONE = 0.5
BETA_TWO = 0.5
EPS_ADAM = 1e-08
DECAY = 0.1
NORM_RATE = 0.3

AXES = ("expert", "head")
F32 = jnp.float32
BF16 = jnp.bfloat16
VMEM_BYTES = 62 * 2**20
MESH = pl.DeviceIdType.MESH


def adam_step(master, first_state, square, gradient, step_rate):
    momentum = BETA_ONE * first_state + (1.0 - BETA_ONE) * gradient
    variance = BETA_TWO * square + (1.0 - BETA_TWO) * gradient * gradient
    first_fix = momentum / (1.0 - BETA_ONE**STEP)
    second_fix = variance / (1.0 - BETA_TWO**STEP)
    updated = master - step_rate * (first_fix / (jnp.sqrt(second_fix) + EPS_ADAM) + DECAY * master)
    return (updated, momentum, variance, updated.astype(BF16))


def dot_nn(a, b):
    return lax.dot_general(a, b, (((1,), (0,)), ((), ())), preferred_element_type=F32)


def dot_nt(a, b):
    return lax.dot_general(a, b, (((1,), (1,)), ((), ())), preferred_element_type=F32)


def dot_tn(a, b):
    return lax.dot_general(a, b, (((0,), (0,)), ((), ())), preferred_element_type=F32)


def cost(microseconds):
    return pl.CostEstimate(
        flops=int(microseconds * 1.1e9), bytes_accessed=int(microseconds * 3e6), transcendentals=0
    )


def params(**kw):
    return pltpu.CompilerParams(vmem_limit_bytes=VMEM_BYTES, **kw)


def route(part, wide_ref, tall_ref, wide_out, tall_out, experts, cap):
    tokens = wide_ref.shape[1]
    row = lax.broadcasted_iota(jnp.int32, (tokens, tokens), 0)
    col = lax.broadcasted_iota(jnp.int32, (tokens, tokens), 1)

    wide = wide_ref[...] ^ part
    names = lax.broadcasted_iota(jnp.int32, (experts, tokens), 0)
    first, second = wide[0:1, :] == names, wide[1:2, :] == names
    seen = (first | second).astype(F32)
    before = dot_nn(seen.astype(BF16), (row < col).astype(BF16))
    place = jnp.concatenate(
        [
            jnp.sum(jnp.where(first, before, 0.0), axis=0, keepdims=True),
            jnp.sum(jnp.where(second, before, 0.0), axis=0, keepdims=True),
        ],
        axis=0,
    ).astype(jnp.int32)
    wide_out[...] = jnp.where(wide_ref[...] < 0, -1, wide * cap + place)

    tall = tall_ref[...] ^ part
    names = lax.broadcasted_iota(jnp.int32, (tokens, experts), 1)
    first, second = tall[:, 0:1] == names, tall[:, 1:2] == names
    seen = (first | second).astype(F32)
    before = dot_nn((col < row).astype(BF16), seen.astype(BF16))
    place = jnp.concatenate(
        [
            jnp.sum(jnp.where(first, before, 0.0), axis=1, keepdims=True),
            jnp.sum(jnp.where(second, before, 0.0), axis=1, keepdims=True),
        ],
        axis=1,
    ).astype(jnp.int32)
    tall_out[...] = jnp.where(tall_ref[...] < 0, -1, tall * cap + place).reshape(tall_out.shape)


def spread_images(stage, rows, out_ref):
    stage[0 : rows.shape[0], :] = rows.astype(F32)
    at = lax.broadcasted_iota(jnp.int32, (PAD, 1), 0)
    for i in range(out_ref.shape[0]):
        image = stage[i * SEQ : i * SEQ + PAD, :]
        out_ref[i] = jnp.where(at < SEQ, image, 0.0).astype(BF16)


def where_am_i(experts):
    quarter = experts // 4
    at_expert, at_head = lax.axis_index("expert"), lax.axis_index("head")
    half = lax.div(at_expert, experts // 2)
    rest = lax.rem(at_expert, experts // 2)
    a = lax.div(rest, quarter)
    b = lax.rem(lax.div(at_head, 2) + a + half, 2)
    return a * 2 * quarter + b * quarter + lax.rem(rest, quarter), half, lax.rem(at_head, 2)


def flipped(experts, part, k):
    there, bit = jnp.int32(0), 1
    while bit < experts:
        there = there + lax.rem(lax.div(part, bit) + lax.div(jnp.int32(k), bit), 2) * bit
        bit = bit * 2
    return there


def partner(experts, part, half, low, k):
    quarter = experts // 4
    there = flipped(experts, part, k)
    a = lax.div(there, 2 * quarter)
    row = half * (experts // 2) + a * quarter + lax.rem(there, quarter)
    return (row, lax.rem(lax.div(there, quarter) + a + half, 2) * 2 + low)


def sequence(experts):
    far = experts // 2
    return [0] + list(range(far, experts)) + list(range(far - 1, 0, -1))


def block_at(experts, j):
    block = jnp.int32(0)
    for i, k in enumerate(sequence(experts)):
        block = jnp.where(j == i, k, block)
    return block


def early_parts(experts):
    turns = sequence(experts)
    last = turns[experts // 2]
    first = [k for k in turns[experts // 2 - 1 :] if k != last]
    rest = [k for k in turns if k and k != last and k not in first]
    return first, rest[::-1], [last], []


def greet(devices):
    barrier = pltpu.get_barrier_semaphore()
    for device in devices:
        pl.semaphore_signal(barrier, inc=1, device_id=device, device_id_type=MESH)
    pl.semaphore_wait(barrier, len(devices))


def picked_rows(wide_ref, rows, k, cap):
    slot = lax.broadcasted_iota(jnp.int32, (cap, rows.shape[0]), 0)
    first = wide_ref[0:1, :] - k * cap
    second = wide_ref[1:2, :] - k * cap
    pick = ((first == slot) | (second == slot)).astype(F32).astype(BF16)
    return dot_nn(pick, rows).astype(BF16)


def my_bits(count, index):
    return [lax.rem(lax.div(index, 2 ** (count - 1 - d)), 2) for d in range(count)]


def across(bits, low, d):
    place = jnp.int32(0)
    for i, bit in enumerate(bits):
        place = place * 2 + (1 - bit if i == d else bit)
    place = place * 2 + low
    return (lax.div(place, 4), lax.rem(place, 4))


def region(bits, full, d=None, flipped=False):
    return tuple(
        slice(None) if i in full else (1 - bit if (flipped and i == d) else bit)
        for i, bit in enumerate(bits)
    )


def parts_of(half_width):
    tiles = half_width // 128
    first = -(-tiles // 2) * 128
    return (slice(0, first), slice(first, half_width))


def gather_steps(
    own_ref, twin, wall, twin_sem, step_send, step_recv, pass_send, pass_recv, between
):
    at_expert, at_head = lax.axis_index("expert"), lax.axis_index("head")
    low = lax.rem(at_head, 2)
    count = wall.ndim - 3
    bits = my_bits(count, lax.div(at_expert * 4 + at_head, 2))
    sibling = (at_expert, at_head + 1 - 2 * low)
    twin_copy = pltpu.make_async_remote_copy(
        src_ref=own_ref,
        dst_ref=twin,
        send_sem=twin_sem.at[0],
        recv_sem=twin_sem.at[1],
        device_id=sibling,
        device_id_type=MESH,
    )
    twin_copy.start()
    half_width = wall.shape[-1]
    cols = parts_of(half_width)
    orders = (list(range(count)), list(range(count - 2)) + [count - 1, count - 2])

    def step_copy(q, i):
        full, d = set(orders[q][:i]), orders[q][i]
        at = (low,) + region(bits, full) + (slice(None), cols[q])
        return pltpu.make_async_remote_copy(
            src_ref=wall.at[at],
            dst_ref=wall.at[at],
            send_sem=step_send.at[q, i],
            recv_sem=step_recv.at[q, i],
            device_id=across(bits, low, d),
            device_id_type=MESH,
        )

    def pass_copy(q, i):
        full, d = set(orders[q][:i]), orders[q][i]
        at = (low,) + region(bits, full, d, True) + (slice(None), cols[q])
        return pltpu.make_async_remote_copy(
            src_ref=wall.at[at],
            dst_ref=wall.at[at],
            send_sem=pass_send.at[q, i],
            recv_sem=pass_recv.at[q, i],
            device_id=sibling,
            device_id_type=MESH,
        )

    between(-1)
    twin_copy.wait()
    first = low == 0
    for side in range(2):
        at = slice(side * half_width, (side + 1) * half_width)
        ours, theirs = own_ref[:, at], twin[:, at]
        wall[(side,) + tuple(bits)] = jnp.concatenate(
            [jnp.where(first, ours, theirs), jnp.where(first, theirs, ours)], axis=0
        ).astype(BF16)
    for i in range(count):
        for q in range(2):
            if i:
                step_copy(q, i - 1).wait_recv()
            step_copy(q, i).start()
        for q in range(2):
            if i:
                pass_copy(q, i - 1).start()
        between(i)
    for q in range(2):
        step_copy(q, count - 1).wait_recv()
        pass_copy(q, count - 1).start()
    for i in range(count):
        for q in range(2):
            step_copy(q, i).wait_send()
            pass_copy(q, i).wait()


def is_me(device):
    return (device[0] == lax.axis_index("expert")) & (device[1] == lax.axis_index("head"))


def hosts(experts):
    at_expert, at_head = lax.axis_index("expert"), lax.axis_index("head")
    part, half, low = where_am_i(experts)
    quarter = experts // 4
    a, b = lax.div(at_expert, 2 * quarter), lax.rem(lax.div(at_expert, quarter), 2)
    out = []
    for k in range(2):
        r = lax.rem(lax.div(at_head, 2) + k, 2)
        row = r * 2 * quarter + a * quarter + lax.rem(at_expert, quarter)
        there = (row, lax.rem(a + b + r, 2) * 2 + low)
        back = (part, lax.rem(half + k, 2) * 2 + low)
        out.append((there, back))
    return out


def start_far_first(experts, copies):
    half = where_am_i(experts)[1]
    at = lax.rem(lax.div(lax.axis_index("head"), 2) + half, 2)
    for turn in range(2):
        for k in range(2):

            @pl.when(lax.rem(at + k + turn, 2) == 1)
            def _(k=k):
                for copy in copies[k]:
                    copy[0]()


def maybe_remote(src, dst, send_sem, recv_sem, device, pieces=1):
    same = is_me(device)
    rows = src.shape[0] // pieces

    def remote(rows_at=None):
        return pltpu.make_async_remote_copy(
            src_ref=src if rows_at is None else src.at[rows_at],
            dst_ref=dst if rows_at is None else dst.at[rows_at],
            send_sem=send_sem,
            recv_sem=recv_sem,
            device_id=device,
            device_id_type=MESH,
        )

    def start():
        @pl.when(same)
        def _():
            pltpu.make_async_copy(src, dst, recv_sem).start()

        @pl.when(jnp.logical_not(same))
        def _():
            for i in range(pieces):
                remote(pl.ds(i * rows, rows)).start()

    def arrived():
        @pl.when(same)
        def _():
            pltpu.make_async_copy(src, dst, recv_sem).wait()

        @pl.when(jnp.logical_not(same))
        def _():
            remote().wait_recv()

    def sent():
        @pl.when(jnp.logical_not(same))
        def _():
            remote().wait_send()

    return start, arrived, sent


def owners_of(experts):
    at_expert, at_head = lax.axis_index("expert"), lax.axis_index("head")
    part, half, low = where_am_i(experts)
    quarter = experts // 4
    x = lax.div(at_head, 2)
    a, b = lax.div(at_expert, 2 * quarter), lax.rem(lax.div(at_expert, quarter), 2)
    rest = a * quarter + lax.rem(at_expert, quarter)
    r = lax.rem(x + a + b, 2)
    return dict(
        slot=lax.rem(x + half, 2),
        beside=(at_expert, (1 - x) * 2 + low),
        direct_to=(part, at_head),
        passed_to=(flipped(experts, part, quarter), at_head),
        direct_from=(r * 2 * quarter + rest, at_head),
        passed_from=((1 - r) * 2 * quarter + rest, at_head),
    )


def reduce_steps(
    all_ref,
    out_ref,
    total,
    last,
    spare,
    pair_sem,
    step_send,
    step_recv,
    last_sem,
    landings,
    between,
):
    at_expert, at_head = lax.axis_index("expert"), lax.axis_index("head")
    low = lax.rem(at_head, 2)
    count = all_ref.ndim - 3
    bits = my_bits(count, lax.div(at_expert * 4 + at_head, 2))
    sibling = (at_expert, at_head + 1 - 2 * low)
    half_width = all_ref.shape[-1]
    cols = parts_of(half_width)
    backwards = list(range(count))[::-1]
    orders = (backwards, [backwards[1], backwards[0]] + backwards[2:])

    def pair_copy(q):
        at = (slice(None),) * count + (slice(None), cols[q])
        return pltpu.make_async_remote_copy(
            src_ref=all_ref.at[(1 - low,) + at],
            dst_ref=total.at[at],
            send_sem=pair_sem.at[q],
            recv_sem=pair_sem.at[2 + q],
            device_id=sibling,
            device_id_type=MESH,
        )

    def step_copy(q, i):
        gone, d = orders[q][:i], orders[q][i]
        full = set(range(count)) - set(gone) - {d}
        at = region(bits, full, d, True) + (slice(None), cols[q])
        return pltpu.make_async_remote_copy(
            src_ref=total.at[at],
            dst_ref=landings[q * count + i],
            send_sem=step_send.at[q, i],
            recv_sem=step_recv.at[q, i],
            device_id=across(bits, low, d),
            device_id_type=MESH,
        )

    for q in range(2):
        pair_copy(q).start()
    for q in range(2):
        at = (slice(None),) * count + (slice(None), cols[q])
        pair_copy(q).wait_recv()
        total[at] = (all_ref[(low,) + at].astype(F32) + total[at].astype(F32)).astype(BF16)
        step_copy(q, 0).start()
    for i in range(count):
        between(i)
        for q in range(2):
            step_copy(q, i).wait_recv()
            gone, d = orders[q][:i], orders[q][i]
            full = set(range(count)) - set(gone) - {d}
            at = region(bits, full) + (slice(None), cols[q])
            added = total[at].astype(F32) + landings[q * count + i][...].astype(F32)
            if i < count - 1:
                total[at] = added.astype(BF16)
                step_copy(q, i + 1).start()
            else:
                last[:, cols[q]] = added
    own_rows = out_ref.shape[0]
    top, bottom = last[0:own_rows, :], last[own_rows:, :]
    first = low == 0
    spare[0] = jnp.where(first, bottom, top)
    last_copy = pltpu.make_async_remote_copy(
        src_ref=spare.at[0],
        dst_ref=spare.at[1],
        send_sem=last_sem.at[0],
        recv_sem=last_sem.at[1],
        device_id=sibling,
        device_id_type=MESH,
    )
    last_copy.start()
    ours = jnp.where(first, top, bottom)
    last_copy.wait()
    theirs = spare[1]
    out_ref[:, 0:half_width] = jnp.where(first, ours, theirs)
    out_ref[:, half_width:] = jnp.where(first, theirs, ours)
    for q in range(2):
        pair_copy(q).wait_send()
        for i in range(count):
            step_copy(q, i).wait_send()


def norm_parts(values):
    centered = values - jnp.mean(values, axis=-1, keepdims=True)
    spread = lax.rsqrt(jnp.mean(centered * centered, axis=-1, keepdims=True) + EPS_NORM)
    return centered * spread, spread


def norm_back(grad, unit, spread, gain):
    scaled = grad * gain
    return spread * (
        scaled
        - jnp.mean(scaled, axis=-1, keepdims=True)
        - unit * jnp.mean(scaled * unit, axis=-1, keepdims=True)
    )


def cut(wall, side, start, stop):
    rows = wall[(side,) + (slice(None),) * (wall.ndim - 2) + (slice(start, stop),)]
    return rows.reshape(-1, stop - start)


def forward_kernel(
    x_ref,
    own_ref,
    wide_in,
    tall_in,
    gy_in,
    inner_ref,
    outer_ref,
    qkv_ref,
    o_ref,
    h_ref,
    n2_ref,
    p_ref,
    out_ref,
    wall_ref,
    w_ref,
    x_out,
    gy_out,
    wide_ref,
    tall_ref,
    small,
    stage,
    masters,
    both_ref,
    held,
    twin,
    wall,
    twin_sem,
    step_send,
    step_recv,
    pass_send,
    pass_recv,
    send_sem,
    recv_sem,
    w_send,
    w_recv,
    sib_send,
    sib_recv,
    own_sem,
    load_sem,
    *,
    experts,
    cap,
):
    width = x_ref.shape[1]
    part, half, low = where_am_i(experts)
    at_expert, at_head = lax.axis_index("expert"), lax.axis_index("head")
    sibling = (at_expert, at_head + 1 - 2 * low)
    count = wall.ndim - 3
    bits = my_bits(count, lax.div(at_expert * 4 + at_head, 2))

    def swap_copy(k):
        return pltpu.make_async_remote_copy(
            src_ref=held.at[k],
            dst_ref=out_ref.at[k],
            send_sem=send_sem.at[k],
            recv_sem=recv_sem.at[k],
            device_id=partner(experts, part, half, low, k),
            device_id_type=MESH,
        )

    pieces = w_send.shape[0] // 2
    piece = 2 * width // pieces

    def sib_copy(k, j):
        at = pl.ds(j * piece, piece)
        return pltpu.make_async_remote_copy(
            src_ref=w_ref.at[k, at],
            dst_ref=w_ref.at[2 + k, at],
            send_sem=sib_send.at[k * pieces + j],
            recv_sem=sib_recv.at[k * pieces + j],
            device_id=sibling,
            device_id_type=MESH,
        )

    w_copies = [
        [
            maybe_remote(
                both_ref.at[pl.ds(j * piece, piece)],
                w_ref.at[k, pl.ds(j * piece, piece)],
                w_send.at[k * pieces + j],
                w_recv.at[k * pieces + j],
                there,
                2,
            )
            for j in range(pieces)
        ]
        for k, (there, _) in enumerate(hosts(experts))
    ]
    early = early_parts(experts)
    own_copy = pltpu.make_async_copy(held.at[0], out_ref.at[0], own_sem.at[0])
    wall_copy = pltpu.make_async_copy(wall, wall_ref, own_sem.at[1])

    @pl.when(pl.program_id(0) == 0)
    def _():
        loads = [
            pltpu.make_async_copy(ref, masters.at[pl.ds(j * width, width), :], load_sem.at[j])
            for j, ref in enumerate((inner_ref, outer_ref))
        ]
        for load in loads:
            load.start()
        greet(
            [sibling]
            + [across(bits, low, d) for d in range(count)]
            + [partner(experts, part, half, low, k) for k in range(1, experts)]
            + [device for pair in hosts(experts) for device in pair]
        )

        def send_blocks(blocks):
            rows = gy_out[...].reshape(-1, width)
            for k in blocks:
                held[k] = picked_rows(wide_ref, rows, k, cap)
                (swap_copy(k) if k else own_copy).start()

        def between(i):
            if i < 0:
                route(part, wide_in, tall_in, wide_ref, tall_ref, experts, cap)
            if i == 0:
                for load in loads:
                    load.wait()
                both_ref[...] = masters[...].astype(BF16)
                spread_images(stage, gy_in[...], gy_out)
            if 0 <= i < len(early):
                send_blocks(early[i])
            if i == 1:
                start_far_first(experts, w_copies)
            if i == 2:
                spread_images(stage, x_ref[...], x_out)

        gather_steps(
            own_ref, twin, wall, twin_sem, step_send, step_recv, pass_send, pass_recv, between
        )
        wall_copy.start()
        send_blocks([0])
        small[...] = cut(wall, 0, 2 * width, 2 * width + 128).astype(F32).T

    x = x_out[pl.program_id(0)].astype(F32)
    gain, shift = small[experts : experts + 1, :], small[experts + 1 : experts + 2, :]
    unit, _ = norm_parts(x)
    n1 = (unit * gain + shift).astype(BF16)
    for j in range(3):
        qkv_ref[0, :, j * width : (j + 1) * width] = dot_nn(
            n1, cut(wall, j // 2, (j % 2) * width, (j % 2 + 1) * width)
        ).astype(BF16)
    lane = lax.broadcasted_iota(jnp.int32, (PAD, 128), 1)
    key_at = lax.broadcasted_iota(jnp.int32, (PAD, PAD), 1)
    for pair in range(width // 128):
        q = qkv_ref[0, :, pair * 128 : (pair + 1) * 128]
        k = qkv_ref[0, :, width + pair * 128 : width + (pair + 1) * 128]
        v = qkv_ref[0, :, 2 * width + pair * 128 : 2 * width + (pair + 1) * 128]
        halves = []
        for side in range(2):
            mine = (lane < HD) if side == 0 else (lane >= HD)
            scores = dot_nt(jnp.where(mine, q, jnp.zeros_like(q)), k) * (HD**-0.5)
            scores = jnp.where(key_at < SEQ, scores, -1e30)
            expo = jnp.exp(scores - jnp.max(scores, axis=-1, keepdims=True))
            probs = expo / jnp.sum(expo, axis=-1, keepdims=True)
            halves.append(dot_nn(probs.astype(BF16), v))
        o_ref[0, :, pair * 128 : (pair + 1) * 128] = jnp.where(
            lane < HD, halves[0], halves[1]
        ).astype(BF16)
    h = x + dot_nn(o_ref[0], cut(wall, 1, width, 2 * width))
    h_ref[0] = h
    gain, shift = small[experts + 2 : experts + 3, :], small[experts + 3 : experts + 4, :]
    unit, _ = norm_parts(h)
    n2 = (unit * gain + shift).astype(BF16)
    n2_ref[0] = n2
    logits = dot_nt(small[0:experts, :].astype(BF16), n2)
    expo = jnp.exp(logits - jnp.max(logits, axis=0, keepdims=True))
    p_ref[0] = expo / jnp.sum(expo, axis=0, keepdims=True)

    @pl.when(pl.program_id(0) == pl.num_programs(0) - 1)
    def _():
        for j in range(pieces):
            for k in range(2):
                w_copies[k][j][1]()
                sib_copy(k, j).start()
        for k in sum(early, []):
            swap_copy(k).wait()
        own_copy.wait()
        wall_copy.wait()
        for j in range(pieces):
            for k in range(2):
                w_copies[k][j][2]()
                sib_copy(k, j).wait()


def expert_kernel(
    wide_ref,
    rows_ref,
    g_ref,
    w_ref,
    router_ref,
    y_ref,
    dr_ref,
    pair_ref,
    x_all,
    g_all,
    held,
    w_all,
    acc,
    y_acc,
    dr_acc,
    x_send,
    x_recv,
    y_sem,
    dr_send,
    dr_recv,
    g_sem,
    w_sem,
    own_sem,
    pair_sem,
    ready_sem,
    *,
    experts,
    cap,
    group,
):
    part, half, low = where_am_i(experts)
    at_expert, at_head = lax.axis_index("expert"), lax.axis_index("head")
    sibling = (at_expert, at_head + 1 - 2 * low)
    greet([partner(experts, part, half, low, k) for k in range(1, experts)] + [sibling])
    width = x_all.shape[2]
    slice_width = w_all.shape[2]
    tile = group * cap

    def x_copy(k):
        return pltpu.make_async_remote_copy(
            src_ref=held.at[k],
            dst_ref=x_all.at[k, pl.ds(0, cap), :],
            send_sem=x_send.at[k],
            recv_sem=x_recv.at[k],
            device_id=partner(experts, part, half, low, k),
            device_id_type=MESH,
        )

    def y_copy(k):
        return pltpu.make_async_copy(g_all.at[k], y_ref.at[k], y_sem.at[k])

    def dr_copy(k):
        return pltpu.make_async_remote_copy(
            src_ref=x_all.at[k],
            dst_ref=dr_ref.at[k],
            send_sem=dr_send.at[k],
            recv_sem=dr_recv.at[k],
            device_id=partner(experts, part, half, low, k),
            device_id_type=MESH,
        )

    weights = [
        pltpu.make_async_copy(w_ref.at[j], w_all.at[j], w_sem.at[j]) for j in range(4)
    ]
    for copy in weights:
        copy.start()
    g_copy = pltpu.make_async_copy(g_ref, g_all, g_sem)
    g_copy.start()
    rows = rows_ref[...]
    turns = sequence(experts)
    for k in turns:
        if k:
            held[k] = picked_rows(wide_ref, rows, k, cap)
            x_copy(k).start()
    x_all[0, 0:cap, :] = picked_rows(wide_ref, rows, 0, cap)
    acc[...] = jnp.zeros_like(acc)
    g_copy.wait()
    for copy in weights:
        copy.wait()

    def one_tile(t, _):
        base = t * group
        names = [block_at(experts, base + j) for j in range(group)]
        for k in names:

            @pl.when(k > 0)
            def _(k=k):
                x_copy(k).wait_recv()

        x = jnp.concatenate([x_all[k, 0:cap, :] for k in names], axis=0)
        g = jnp.concatenate([g_all[k] for k in names], axis=0)
        logits = dot_nt(x, router_ref[...])
        expo = jnp.exp(logits - jnp.max(logits, axis=-1, keepdims=True))
        probs = expo / jnp.sum(expo, axis=-1, keepdims=True)
        name = lax.broadcasted_iota(jnp.int32, probs.shape, 1)
        gate = jnp.sum(jnp.where(name == part, probs, 0.0), axis=-1, keepdims=True)
        dy = (gate * g.astype(F32)).astype(BF16)
        x_turned, dy_turned = x.T, dy.T

        def first(s):
            w_in = w_all[s, 0:width, :]
            w_out = w_all[s, width : 2 * width, :]
            acts, dus = [], []
            for i in range(0, slice_width, 256):
                u = dot_nn(x, w_in[:, i : i + 256])
                da = dot_nt(dy, w_out[i : i + 256, :])
                root = 0.7978845608028654
                sq = u * u
                th = jnp.tanh(u * (root + (root * 0.044715) * sq))
                plus = 0.5 + 0.5 * th
                acts.append((u * plus).astype(BF16))
                slope = plus + (0.5 * u) * (1.0 - th * th) * (root + (3.0 * root * 0.044715) * sq)
                dus.append((da * slope).astype(BF16))
            return jnp.concatenate(acts, axis=1), jnp.concatenate(dus, axis=1), w_in, w_out

        def second(s, fresh, act, du, w_in, w_out):
            y_part, dr_part = dot_nn(act, w_out), dot_nt(du, w_in)
            y_acc[...] = y_part if fresh else y_acc[...] + y_part
            dr_acc[...] = dr_part if fresh else dr_acc[...] + dr_part
            acc[s, 0] += dot_nn(x_turned, du)
            acc[s, 1] += dot_nn(dy_turned, act)

        order = (2, 3, 0, 1)
        kept = first(order[0])
        for i in range(1, 4):
            fresh = first(order[i])
            second(order[i - 1], i == 1, *kept)
            kept = fresh
        second(order[3], False, *kept)

        y = y_acc[...]
        dgate = jnp.sum(g.astype(F32) * y, axis=-1, keepdims=True)
        dr_low, y_low = dr_acc[...].astype(BF16), (gate * y).astype(BF16)
        for j, k in enumerate(names):
            x_all[k, 0:cap, :] = dr_low[j * cap : (j + 1) * cap, :]
            g_all[k] = y_low[j * cap : (j + 1) * cap, :]
            line = jnp.broadcast_to(dgate[j * cap : (j + 1) * cap, :], (cap, 128))
            if cap % 128:
                line = jnp.concatenate([line, jnp.zeros((128 - cap % 128, 128), F32)], axis=0)
            line = line.T[0:1, :]
            top = line.astype(BF16).astype(F32)
            middle = (line - top).astype(BF16).astype(F32)
            last = line - top - middle
            long = line.shape[1]
            meta = jnp.concatenate([top, middle, last, jnp.zeros((13, long), F32)], axis=0)
            meta = jnp.concatenate([meta, jnp.zeros((16, width - long), F32)], axis=1)
            x_all[k, cap : cap + 16, :] = meta.astype(BF16)

        for k in names:

            @pl.when(k > 0)
            def _(k=k):
                dr_copy(k).start()

            @pl.when(k == 0)
            def _():
                pltpu.make_async_copy(x_all.at[0], dr_ref.at[0], own_sem).start()

            y_copy(k).start()

        return 0

    lax.fori_loop(0, experts // group, one_tile, 0)

    pl.semaphore_signal(ready_sem, inc=1, device_id=sibling, device_id_type=MESH)
    for j in range(2):
        for side in range(2):
            w_all[j, side * width : (side + 1) * width, :] = acc[2 + j, side].astype(BF16)
    pl.semaphore_wait(ready_sem, 1)
    swaps = [
        pltpu.make_async_remote_copy(
            src_ref=w_all.at[j],
            dst_ref=w_all.at[2 + j],
            send_sem=pair_sem.at[j],
            recv_sem=pair_sem.at[2 + j],
            device_id=sibling,
            device_id_type=MESH,
        )
        for j in range(2)
    ]
    for copy in swaps:
        copy.start()
    results = []
    for j in range(2):
        swaps[j].wait()
        for side in range(2):
            at = slice(side * width, (side + 1) * width)
            w_all[2 + j, at, :] = (w_all[2 + j, at, :].astype(F32) + acc[j, side]).astype(BF16)
        results.append(pltpu.make_async_copy(w_all.at[2 + j], pair_ref.at[j], w_sem.at[j]))
        results[-1].start()
    for copy in results:
        copy.wait()

    def settle(k, _):
        x_copy(k).wait_send()
        dr_copy(k).wait()
        y_copy(k).wait()
        return 0

    lax.fori_loop(1, experts, settle, 0)
    y_copy(0).wait()
    pltpu.make_async_copy(x_all.at[0], dr_ref.at[0], own_sem).wait()


def backward_kernel(
    tall_ref,
    gy_ref,
    x_ref,
    h_ref,
    qkv_ref,
    o_ref,
    p_ref,
    wall_ref,
    dr_ref,
    y_ref,
    pair_ref,
    grad_ref,
    out_ref,
    shared_ref,
    back_ref,
    beside_ref,
    small,
    acc,
    small_acc,
    dqkv,
    dp_all,
    y_in,
    send_sem,
    recv_sem,
    own_sem,
    g_send,
    g_recv,
    all_ref,
    total,
    last,
    spare,
    pair_sem,
    step_send,
    step_recv,
    last_sem,
    *landings,
    experts,
    cap,
):
    width = x_ref.shape[2]
    part, half, low = where_am_i(experts)
    step = pl.program_id(0)

    def swap_copy(k):
        return pltpu.make_async_remote_copy(
            src_ref=y_ref.at[k],
            dst_ref=y_in.at[k],
            send_sem=send_sem.at[k],
            recv_sem=recv_sem.at[k],
            device_id=partner(experts, part, half, low, k),
            device_id_type=MESH,
        )

    own_copy = pltpu.make_async_copy(y_ref.at[0], y_in.at[0], own_sem)
    at_expert, at_head = lax.axis_index("expert"), lax.axis_index("head")
    sibling = (at_expert, at_head + 1 - 2 * low)
    count = all_ref.ndim - 3
    bits = my_bits(count, lax.div(at_expert * 4 + at_head, 2))
    ways = owners_of(experts)
    slot_at = ways["slot"]
    direct = maybe_remote(
        pair_ref.at[slot_at],
        back_ref.at[slot_at],
        g_send.at[0],
        g_recv.at[0],
        ways["direct_to"],
        12,
    )
    turns = beside_ref.shape[0]
    piece = beside_ref.shape[1]
    aside = [
        pltpu.make_async_remote_copy(
            src_ref=pair_ref.at[1 - slot_at, pl.ds(j * piece, piece)],
            dst_ref=beside_ref.at[j],
            send_sem=g_send.at[1 + j],
            recv_sem=g_recv.at[1 + j],
            device_id=ways["beside"],
            device_id_type=MESH,
        )
        for j in range(turns)
    ]
    passed = [
        maybe_remote(
            beside_ref.at[j],
            back_ref.at[slot_at, pl.ds(j * piece, piece)],
            g_send.at[1 + turns + j],
            g_recv.at[1 + turns + j],
            ways["passed_to"],
            3,
        )
        for j in range(turns)
    ]

    @pl.when(step == 0)
    def _():
        greet(
            [sibling, ways["beside"]]
            + [across(bits, low, d) for d in range(count)]
            + [partner(experts, part, half, low, k) for k in range(1, experts)]
            + [ways["direct_to"], ways["passed_to"], ways["direct_from"], ways["passed_from"]]
        )
        for j in range(turns):
            aside[j].start()
        direct[0]()
        own_copy.start()
        small[...] = wall_ref[0, :, 2 * width :].astype(F32).T
        acc[...] = jnp.zeros_like(acc)
        small_acc[...] = jnp.zeros_like(small_acc)

    gy = gy_ref[0].astype(F32)
    h = h_ref[step]
    unit, spread = norm_parts(h)
    gain, shift = small[experts + 2 : experts + 3, :], small[experts + 3 : experts + 4, :]
    n2 = (unit * gain + shift).astype(BF16)
    slot = lax.broadcasted_iota(jnp.int32, (PAD, cap), 1)

    def owners(image, k):
        first = tall_ref[image, :, 0:1] - k * cap
        second = tall_ref[image, :, 1:2] - k * cap
        return ((first == slot) | (second == slot)).astype(F32).astype(BF16)

    dn2 = jnp.zeros((PAD, width), F32)
    for k in range(experts):
        pick = owners(step, k)
        dn2 = dn2 + dot_nn(pick, dr_ref[k, 0:cap, :])
        line = dot_nt(dr_ref[k, cap : cap + 16, 0:cap], pick)
        dp_all[pl.ds(flipped(experts, part, k), 1), :] = (
            line[0:1, :] + line[1:2, :] + line[2:3, :]
        )
    probs = p_ref[0]
    dp = dp_all[...]
    dlogits = (probs * (dp - jnp.sum(dp * probs, axis=0, keepdims=True))).astype(BF16)
    small_acc[0:experts, :] += dot_nn(dlogits, n2)
    dn2 = dn2 + dot_tn(dlogits, small[0:experts, :].astype(BF16))
    small_acc[experts + 2 : experts + 3, :] += jnp.sum(dn2 * unit, axis=0, keepdims=True)
    small_acc[experts + 3 : experts + 4, :] += jnp.sum(dn2, axis=0, keepdims=True)
    dh = gy + norm_back(dn2, unit, spread, gain)
    dh_low = dh.astype(BF16)
    acc[0:width, 3 * width :] += dot_tn(o_ref[0], dh_low)
    do = dot_nt(dh_low, wall_ref[1, :, width : 2 * width]).astype(BF16)

    lane = lax.broadcasted_iota(jnp.int32, (PAD, 128), 1)
    key_at = lax.broadcasted_iota(jnp.int32, (PAD, PAD), 0)
    for pair in range(width // 128):
        q = qkv_ref[0, :, pair * 128 : (pair + 1) * 128]
        k = qkv_ref[0, :, width + pair * 128 : width + (pair + 1) * 128]
        v = qkv_ref[0, :, 2 * width + pair * 128 : 2 * width + (pair + 1) * 128]
        dop = do[:, pair * 128 : (pair + 1) * 128]
        parts = []
        for side in range(2):
            mine = (lane < HD) if side == 0 else (lane >= HD)
            k_mine = jnp.where(mine, k, jnp.zeros_like(k))
            v_mine = jnp.where(mine, v, jnp.zeros_like(v))
            scores = dot_nt(k_mine, q) * (HD**-0.5)
            scores = jnp.where(key_at < SEQ, scores, -1e30)
            expo = jnp.exp(scores - jnp.max(scores, axis=0, keepdims=True))
            prob = expo / jnp.sum(expo, axis=0, keepdims=True)
            dprob = dot_nt(v_mine, dop)
            dscore = prob * (dprob - jnp.sum(dprob * prob, axis=0, keepdims=True))
            dz = (dscore * (HD**-0.5)).astype(BF16)
            parts.append((dot_tn(dz, k), dot_nn(dz, q), dot_nn(prob.astype(BF16), dop)))
        for j in range(3):
            dqkv[:, j * width + pair * 128 : j * width + (pair + 1) * 128] = jnp.where(
                lane < HD, parts[0][j], parts[1][j]
            ).astype(BF16)

    unit, spread = norm_parts(x_ref[0].astype(F32))
    gain, shift = small[experts : experts + 1, :], small[experts + 1 : experts + 2, :]
    n1 = (unit * gain + shift).astype(BF16)
    dn1 = jnp.zeros((PAD, width), F32)
    for j in range(3):
        cols = slice(j * width, (j + 1) * width)
        acc[0:width, cols] += dot_tn(n1, dqkv[:, cols])
        dn1 = dn1 + dot_nt(
            dqkv[:, cols], wall_ref[j // 2, :, (j % 2) * width : (j % 2 + 1) * width]
        )
    small_acc[experts : experts + 1, :] += jnp.sum(dn1 * unit, axis=0, keepdims=True)
    small_acc[experts + 1 : experts + 2, :] += jnp.sum(dn1, axis=0, keepdims=True)
    grad = dh + norm_back(dn1, unit, spread, gain)
    images = tall_ref.shape[0]
    for i in range(images):

        @pl.when(step == i)
        def _(i=i):
            grad_ref[i * SEQ : (i + 1) * SEQ, :] = grad[0:SEQ, :]

    for j in range(turns):

        @pl.when(step == j)
        def _(j=j):
            aside[j].wait_recv()
            passed[j][0]()
            for k in list(range(experts - 1, 0, -1))[j::turns]:
                swap_copy(k).start()

    @pl.when(step == pl.num_programs(0) - 1)
    def _():
        blocks = all_ref.shape[1:-1]
        everything = (slice(None),) * len(blocks)
        for j in range(4):
            all_ref[(j // 2,) + everything + (slice((j % 2) * width, (j % 2 + 1) * width),)] = (
                acc[0:width, j * width : (j + 1) * width].astype(BF16).reshape(blocks + (width,))
            )
        rest = (slice(2 * width, 2 * width + 128),)
        all_ref[(0,) + everything + rest] = (
            small_acc[...].T.astype(BF16).reshape(blocks + (128,))
        )
        all_ref[(1,) + everything + rest] = jnp.zeros(blocks + (128,), BF16)

        def one_image(image):
            mixed = h_ref[image]
            for k in range(experts):
                mixed = mixed + dot_nn(owners(image, k), y_in[k])
            acc[image * SEQ : (image + 1) * SEQ, 0:width] = mixed[0:SEQ, :]

        def between(i):
            if i == count - 1:
                for k in range(1, experts):
                    swap_copy(k).wait()
                own_copy.wait()
                for image in range(images):
                    one_image(image)
                out_ref[...] = acc[0 : out_ref.shape[0], 0:width].astype(BF16)

        reduce_steps(
            all_ref,
            shared_ref,
            total,
            last,
            spare,
            pair_sem,
            step_send,
            step_recv,
            last_sem,
            landings,
            between,
        )
        for j in range(turns):
            aside[j].wait_send()
            passed[j][1]()
            passed[j][2]()
        direct[1]()
        direct[2]()


def adam_kernel(*refs, rates, shapes):
    ins, outs = refs[: len(refs) - 24], refs[len(refs) - 24 :]
    inner, outer = ins[0:3], ins[3:6]
    a0, a1, b0, b1 = ins[6:10]
    shared = ins[10:22]
    qkv_grad, router_grad, norm_grad, shared_grad = ins[22:26]

    def put(at, masters, grad, rate):
        new = adam_step(*(m[...] for m in masters), grad, rate)
        for j in range(4):
            outs[at + j][...] = new[j]

    put(16, inner, a0[0].astype(F32) + a1[0].astype(F32), rates[4])
    put(20, outer, (b0[0].astype(F32) + b1[0].astype(F32)).T, rates[5])

    @pl.when(pl.program_id(0) == 0)
    def _():
        proj = shapes
        put(0, shared[0:3], qkv_grad[...], rates[0])
        put(4, shared[3:6], shared_grad[:, proj[0] : proj[1]], rates[1])
        put(8, shared[6:9], router_grad[...], rates[2])
        put(12, shared[9:12], norm_grad[...], rates[3])


def on_device(
    expert_axis,
    block_input,
    output_grad,
    routes,
    qkv_master,
    qkv_mean,
    qkv_square,
    proj_master,
    proj_mean,
    proj_square,
    router_master,
    router_mean,
    router_square,
    norm_master,
    norm_mean,
    norm_square,
    inner_master,
    inner_mean,
    inner_square,
    outer_master,
    outer_mean,
    outer_square,
):
    row_count, width = block_input.shape
    heads = width // HD
    images = row_count // SEQ
    tokens = images * PAD
    experts = router_master.shape[1]
    own_rows = qkv_master.shape[0]
    bound = row_count * 16 // (5 * experts) + 1
    cap = -(-bound // 16) * 16
    group = max(1, min(experts, 640 // cap // 2 * 2))
    while experts % group:
        group = group - 1
    slice_width = inner_master.shape[2]
    vmem = pl.BlockSpec(memory_space=pltpu.VMEM)
    smem = pl.BlockSpec(memory_space=pltpu.SMEM)
    anywhere = pl.BlockSpec(memory_space=pl.ANY)
    struct = jax.ShapeDtypeStruct

    qkv_own = qkv_master.reshape(own_rows, heads, 3, HD).transpose(0, 2, 1, 3)
    qkv_own = qkv_own.reshape(own_rows, 3 * width)
    wall_own = jnp.concatenate(
        [
            qkv_own[:, : 2 * width],
            router_master,
            norm_master.T,
            jnp.zeros((own_rows, 128 - experts - 4), F32),
            qkv_own[:, 2 * width :],
            proj_master,
            jnp.zeros((own_rows, 128), F32),
        ],
        axis=1,
    )
    half_width = 2 * width + 128
    count = (width // own_rows).bit_length() - 2
    block = (2,) * count + (2 * own_rows, half_width)

    tall = jnp.pad(
        routes.reshape(images, SEQ, 2), ((0, 0), (0, PAD - SEQ), (0, 0)), constant_values=-1
    ).reshape(tokens, 2)
    dma = pltpu.SemaphoreType.DMA

    def image_spec(*dims):
        return pl.BlockSpec((1,) + dims, lambda i: (i,) + (0,) * len(dims))

    def whole_spec(*dims, once=True):
        mode = dict(pipeline_mode=pl.Buffered(1)) if once else {}
        return pl.BlockSpec(dims, lambda i: (0,) * len(dims), **mode)

    qkv, attended, middle, second, probs, g_blocks, wall, w_all, x, gy, wide_slots, tall_slots = (
        pl.pallas_call(
            functools.partial(forward_kernel, experts=experts, cap=cap),
            grid=(images,),
            out_shape=(
                struct((images, PAD, 3 * width), BF16),
                struct((images, PAD, width), BF16),
                struct((images, PAD, width), F32),
                struct((images, PAD, width), BF16),
                struct((images, experts, PAD), F32),
                struct((experts, cap, width), BF16),
                struct((2,) + block, BF16),
                struct((4, 2 * width, slice_width), BF16),
                struct((images, PAD, width), BF16),
                struct((images, PAD, width), BF16),
                struct((2, tokens), jnp.int32),
                struct((images, PAD, 2), jnp.int32),
            ),
            in_specs=[
                whole_spec(row_count, width),
                whole_spec(*wall_own.shape),
                whole_spec(2, tokens),
                whole_spec(tokens, 2),
                whole_spec(row_count, width),
                anywhere,
                anywhere,
            ],
            out_specs=(
                image_spec(PAD, 3 * width),
                image_spec(PAD, width),
                image_spec(PAD, width),
                image_spec(PAD, width),
                image_spec(experts, PAD),
                anywhere,
                anywhere,
                anywhere,
                whole_spec(images, PAD, width, once=False),
                whole_spec(images, PAD, width, once=False),
                whole_spec(2, tokens, once=False),
                whole_spec(images, PAD, 2, once=False),
            ),
            scratch_shapes=[
                pltpu.VMEM((128, width), F32),
                pltpu.VMEM((tokens, width), F32),
                pltpu.VMEM((2 * width, slice_width), F32),
                pltpu.VMEM((2 * width, slice_width), BF16),
                pltpu.VMEM((experts, cap, width), BF16),
                pltpu.VMEM(wall_own.shape, F32),
                pltpu.VMEM((2,) + block, BF16),
                dma((2,)),
            ]
            + [dma((2, count))] * 4
            + [dma((experts,))] * 2
            + [dma((8,))] * 4
            + [dma((2,))] * 2,
            compiler_params=params(collective_id=0, has_side_effects=True),
            cost_estimate=cost(120),
            name="forward",
        )(
            block_input,
            wall_own,
            tall.T,
            tall,
            output_grad,
            inner_master.reshape(width, slice_width),
            outer_master.reshape(slice_width, width),
        )
    )
    wall = wall.reshape(2, width, half_width)

    router_low = wall[0, :, 2 * width : 2 * width + experts].T
    y_blocks, dr_blocks, grad_pair = pl.pallas_call(
        functools.partial(expert_kernel, experts=experts, cap=cap, group=group),
        out_shape=(
            struct((experts, cap, width), BF16),
            struct((experts, cap + 16, width), BF16),
            struct((2, 2 * width, slice_width), BF16),
        ),
        in_specs=[vmem, vmem, anywhere, anywhere, vmem],
        out_specs=[anywhere] * 3,
        scratch_shapes=[
            pltpu.VMEM((experts, cap + 16, width), BF16),
            pltpu.VMEM((experts, cap, width), BF16),
            pltpu.VMEM((experts, cap, width), BF16),
            pltpu.VMEM((4, 2 * width, slice_width), BF16),
            pltpu.VMEM((4, 2, width, slice_width), F32),
            pltpu.VMEM((group * cap, width), F32),
            pltpu.VMEM((group * cap, width), F32),
        ]
        + [dma((experts,))] * 5
        + [dma, dma((4,)), dma, dma((4,)), pltpu.SemaphoreType.REGULAR],
        compiler_params=params(collective_id=1, has_side_effects=True),
        cost_estimate=cost(140),
        name="experts",
    )(
        wide_slots,
        second.reshape(tokens, width),
        g_blocks,
        w_all,
        router_low,
    )

    landings = [
        pltpu.VMEM((2,) * (count - 1 - i) + (2 * own_rows, c.stop - c.start), BF16)
        for c in parts_of(half_width)
        for i in range(count)
    ]
    input_grad, block_output, shared_own, grad_back, _ = pl.pallas_call(
        functools.partial(backward_kernel, experts=experts, cap=cap),
        grid=(images,),
        out_shape=(
            struct((row_count, width), F32),
            struct((row_count, width), BF16),
            struct((own_rows, 2 * half_width), F32),
            struct((2, 2 * width, slice_width), BF16),
            struct((images, 2 * width // images, slice_width), BF16),
        ),
        in_specs=[
            whole_spec(images, PAD, 2),
            image_spec(PAD, width),
            image_spec(PAD, width),
            whole_spec(images, PAD, width),
            image_spec(PAD, 3 * width),
            image_spec(PAD, width),
            image_spec(experts, PAD),
            whole_spec(2, width, half_width),
            whole_spec(experts, cap + 16, width),
            anywhere,
            anywhere,
        ],
        out_specs=(
            whole_spec(row_count, width),
            whole_spec(row_count, width),
            whole_spec(own_rows, 2 * half_width),
            anywhere,
            anywhere,
        ),
        scratch_shapes=[
            pltpu.VMEM((128, width), F32),
            pltpu.VMEM((max(width, row_count + 7 & -8), 4 * width), F32),
            pltpu.VMEM((128, width), F32),
            pltpu.VMEM((PAD, 3 * width), BF16),
            pltpu.VMEM((experts, PAD), F32),
            pltpu.VMEM((experts, cap, width), BF16),
            dma((experts,)),
            dma((experts,)),
            dma,
            dma((1 + 2 * images,)),
            dma((1 + 2 * images,)),
            pltpu.VMEM((2,) + block, BF16),
            pltpu.VMEM(block, BF16),
            pltpu.VMEM((2 * own_rows, half_width), F32),
            pltpu.VMEM((2, own_rows, half_width), F32),
            dma((4,)),
            dma((2, count)),
            dma((2, count)),
            dma((2,)),
        ]
        + landings,
        compiler_params=params(collective_id=2, has_side_effects=True),
        cost_estimate=cost(120),
        name="backward",
    )(tall_slots, gy, x, middle, qkv, attended, probs, wall, dr_blocks, y_blocks, grad_pair)

    qkv_owned = jnp.concatenate(
        [shared_own[:, : 2 * width], shared_own[:, half_width : half_width + width]], axis=1
    )
    qkv_owned = qkv_owned.reshape(own_rows, 3, heads, HD).transpose(0, 2, 1, 3)
    qkv_owned = qkv_owned.reshape(own_rows, 3 * width)
    small_owned = shared_own[:, 2 * width : 2 * width + experts + 4].T
    small_owned = [small_owned[:experts], small_owned[experts:]]

    rates = (
        2.0 * width ** (-0.5),
        2.0 * (width // 16) ** (-0.5),
        2.0 * (4 * width) ** (-0.5),
        NORM_RATE,
        2.0 * width ** (-0.5),
        2.0 * max(1, FF * 4 // (experts * experts)) ** (-0.5),
    )
    step_rows = 128

    def rows_spec(cols):
        return pl.BlockSpec((step_rows, cols), lambda i: (i, 0))

    shared = [
        qkv_master,
        qkv_mean,
        qkv_square,
        proj_master,
        proj_mean,
        proj_square,
        router_master.T,
        router_mean.T,
        router_square.T,
        norm_master,
        norm_mean,
        norm_square,
    ]
    inner = [v.reshape(width, slice_width) for v in (inner_master, inner_mean, inner_square)]
    outer = [v.reshape(slice_width, width) for v in (outer_master, outer_mean, outer_square)]
    state = []
    for v in shared[::3] + [inner[0], outer[0]]:
        state += [struct(v.shape, t) for t in (F32, F32, F32, BF16)]
    new = pl.pallas_call(
        functools.partial(
            adam_kernel,
            rates=rates,
            shapes=(half_width + width, half_width + 2 * width),
        ),
        grid=(width // step_rows,),
        out_shape=state,
        in_specs=[rows_spec(slice_width)] * 3
        + [rows_spec(width)] * 3
        + [
            pl.BlockSpec((1, step_rows, slice_width), functools.partial(lambda k, i: (k, i, 0), k))
            for k in range(2)
        ]
        + [
            pl.BlockSpec((1, width, step_rows), functools.partial(lambda k, i: (k, 1, i), k))
            for k in range(2)
        ]
        + [whole_spec(*v.shape) for v in shared + [qkv_owned] + small_owned + [shared_own]],
        out_specs=[whole_spec(*v.shape, once=False) for v in state[:16]]
        + [rows_spec(slice_width)] * 4
        + [rows_spec(width)] * 4,
        compiler_params=params(),
        cost_estimate=cost(15),
        name="adam",
    )(*inner, *outer, *([grad_back] * 4), *shared, qkv_owned, *small_owned, shared_own)
    return (
        block_output,
        input_grad,
        *new[:8],
        *(v.T for v in new[8:12]),
        *new[12:16],
        *(v[None] for v in new[16:]),
    )


def solution(mesh):
    rows = P(AXES, None)
    cols = P(None, AXES)
    inner = P("expert", None, "head")
    outer = P("expert", "head", None)
    in_specs = (rows,) * 12 + (cols,) * 3 + (inner,) * 3 + (outer,) * 3
    out_specs = (rows,) * 14 + (cols,) * 4 + (inner,) * 4 + (outer,) * 4
    return jax.shard_map(
        functools.partial(on_device, mesh.shape["expert"]),
        mesh=mesh,
        in_specs=in_specs,
        out_specs=out_specs,
        check_vma=False,
    )
```

```python
import functools

import jax
import jax.numpy as jnp
from jax import lax
from jax.experimental import pallas as pl
from jax.experimental.pallas import tpu as pltpu
from jax.sharding import PartitionSpec as P

HD = 64
FF = 3072
SEQ = 197
PAD = 208
STEP = 3

EPS_NORM = 1e-06
BETA_ONE = 0.5
BETA_TWO = 0.5
EPS_ADAM = 1e-08
DECAY = 0.1
NORM_RATE = 0.3

AXES = ("expert", "head")
F32 = jnp.float32
BF16 = jnp.bfloat16
VMEM_BYTES = 62 * 2**20
MESH = pl.DeviceIdType.MESH


def adam_step(master, first_state, square, gradient, step_rate):
    momentum = BETA_ONE * first_state + (1.0 - BETA_ONE) * gradient
    variance = BETA_TWO * square + (1.0 - BETA_TWO) * gradient * gradient
    first_fix = momentum / (1.0 - BETA_ONE**STEP)
    second_fix = variance / (1.0 - BETA_TWO**STEP)
    updated = master - step_rate * (first_fix / (jnp.sqrt(second_fix) + EPS_ADAM) + DECAY * master)
    return (updated, momentum, variance, updated.astype(BF16))


def dot_nn(a, b):
    return lax.dot_general(a, b, (((1,), (0,)), ((), ())), preferred_element_type=F32)


def dot_nt(a, b):
    return lax.dot_general(a, b, (((1,), (1,)), ((), ())), preferred_element_type=F32)


def dot_tn(a, b):
    return lax.dot_general(a, b, (((0,), (0,)), ((), ())), preferred_element_type=F32)


def cost(microseconds):
    return pl.CostEstimate(
        flops=int(microseconds * 1.1e9), bytes_accessed=int(microseconds * 3e6), transcendentals=0
    )


def params(**kw):
    return pltpu.CompilerParams(vmem_limit_bytes=VMEM_BYTES, **kw)


def route(part, wide_ref, tall_ref, wide_out, tall_out, experts, cap):
    tokens = wide_ref.shape[1]
    row = lax.broadcasted_iota(jnp.int32, (tokens, tokens), 0)
    col = lax.broadcasted_iota(jnp.int32, (tokens, tokens), 1)

    wide = wide_ref[...] ^ part
    names = lax.broadcasted_iota(jnp.int32, (experts, tokens), 0)
    first, second = wide[0:1, :] == names, wide[1:2, :] == names
    seen = (first | second).astype(F32)
    before = dot_nn(seen.astype(BF16), (row < col).astype(BF16))
    place = jnp.concatenate(
        [
            jnp.sum(jnp.where(first, before, 0.0), axis=0, keepdims=True),
            jnp.sum(jnp.where(second, before, 0.0), axis=0, keepdims=True),
        ],
        axis=0,
    ).astype(jnp.int32)
    wide_out[...] = jnp.where(wide_ref[...] < 0, -1, wide * cap + place)

    tall = tall_ref[...] ^ part
    names = lax.broadcasted_iota(jnp.int32, (tokens, experts), 1)
    first, second = tall[:, 0:1] == names, tall[:, 1:2] == names
    seen = (first | second).astype(F32)
    before = dot_nn((col < row).astype(BF16), seen.astype(BF16))
    place = jnp.concatenate(
        [
            jnp.sum(jnp.where(first, before, 0.0), axis=1, keepdims=True),
            jnp.sum(jnp.where(second, before, 0.0), axis=1, keepdims=True),
        ],
        axis=1,
    ).astype(jnp.int32)
    tall_out[...] = jnp.where(tall_ref[...] < 0, -1, tall * cap + place).reshape(tall_out.shape)


def spread_images(stage, rows, out_ref):
    stage[0 : rows.shape[0], :] = rows.astype(F32)
    at = lax.broadcasted_iota(jnp.int32, (PAD, 1), 0)
    for i in range(out_ref.shape[0]):
        image = stage[i * SEQ : i * SEQ + PAD, :]
        out_ref[i] = jnp.where(at < SEQ, image, 0.0).astype(BF16)


def where_am_i(experts):
    quarter = experts // 4
    at_expert, at_head = lax.axis_index("expert"), lax.axis_index("head")
    half = lax.div(at_expert, experts // 2)
    rest = lax.rem(at_expert, experts // 2)
    a = lax.div(rest, quarter)
    b = lax.rem(lax.div(at_head, 2) + a + half, 2)
    return a * 2 * quarter + b * quarter + lax.rem(rest, quarter), half, lax.rem(at_head, 2)


def flipped(experts, part, k):
    there, bit = jnp.int32(0), 1
    while bit < experts:
        there = there + lax.rem(lax.div(part, bit) + lax.div(jnp.int32(k), bit), 2) * bit
        bit = bit * 2
    return there


def partner(experts, part, half, low, k):
    quarter = experts // 4
    there = flipped(experts, part, k)
    a = lax.div(there, 2 * quarter)
    row = half * (experts // 2) + a * quarter + lax.rem(there, quarter)
    return (row, lax.rem(lax.div(there, quarter) + a + half, 2) * 2 + low)


def sequence(experts):
    far = experts // 2
    return [0] + list(range(far, experts)) + list(range(far - 1, 0, -1))


def block_at(experts, j):
    block = jnp.int32(0)
    for i, k in enumerate(sequence(experts)):
        block = jnp.where(j == i, k, block)
    return block


def early_parts(experts):
    turns = sequence(experts)
    last = turns[experts // 2]
    first = [k for k in turns[experts // 2 - 1 :] if k != last]
    rest = [k for k in turns if k and k != last and k not in first]
    return first, rest[::-1], [last], []


def greet(devices):
    barrier = pltpu.get_barrier_semaphore()
    for device in devices:
        pl.semaphore_signal(barrier, inc=1, device_id=device, device_id_type=MESH)
    pl.semaphore_wait(barrier, len(devices))


def picked_rows(wide_ref, rows, k, cap):
    slot = lax.broadcasted_iota(jnp.int32, (cap, rows.shape[0]), 0)
    first = wide_ref[0:1, :] - k * cap
    second = wide_ref[1:2, :] - k * cap
    pick = ((first == slot) | (second == slot)).astype(F32).astype(BF16)
    return dot_nn(pick, rows).astype(BF16)


def my_bits(count, index):
    return [lax.rem(lax.div(index, 2 ** (count - 1 - d)), 2) for d in range(count)]


def across(bits, low, d):
    place = jnp.int32(0)
    for i, bit in enumerate(bits):
        place = place * 2 + (1 - bit if i == d else bit)
    place = place * 2 + low
    return (lax.div(place, 4), lax.rem(place, 4))


def region(bits, full, d=None, flipped=False):
    return tuple(
        slice(None) if i in full else (1 - bit if (flipped and i == d) else bit)
        for i, bit in enumerate(bits)
    )


def parts_of(half_width):
    tiles = half_width // 128
    first = -(-tiles // 2) * 128
    return (slice(0, first), slice(first, half_width))


def gather_steps(
    own_ref, twin, wall, twin_sem, step_send, step_recv, pass_send, pass_recv, between
):
    at_expert, at_head = lax.axis_index("expert"), lax.axis_index("head")
    low = lax.rem(at_head, 2)
    count = wall.ndim - 3
    bits = my_bits(count, lax.div(at_expert * 4 + at_head, 2))
    sibling = (at_expert, at_head + 1 - 2 * low)
    twin_copy = pltpu.make_async_remote_copy(
        src_ref=own_ref,
        dst_ref=twin,
        send_sem=twin_sem.at[0],
        recv_sem=twin_sem.at[1],
        device_id=sibling,
        device_id_type=MESH,
    )
    twin_copy.start()
    half_width = wall.shape[-1]
    cols = parts_of(half_width)
    orders = (list(range(count)), list(range(count - 2)) + [count - 1, count - 2])

    def step_copy(q, i):
        full, d = set(orders[q][:i]), orders[q][i]
        at = (low,) + region(bits, full) + (slice(None), cols[q])
        return pltpu.make_async_remote_copy(
            src_ref=wall.at[at],
            dst_ref=wall.at[at],
            send_sem=step_send.at[q, i],
            recv_sem=step_recv.at[q, i],
            device_id=across(bits, low, d),
            device_id_type=MESH,
        )

    def pass_copy(q, i):
        full, d = set(orders[q][:i]), orders[q][i]
        at = (low,) + region(bits, full, d, True) + (slice(None), cols[q])
        return pltpu.make_async_remote_copy(
            src_ref=wall.at[at],
            dst_ref=wall.at[at],
            send_sem=pass_send.at[q, i],
            recv_sem=pass_recv.at[q, i],
            device_id=sibling,
            device_id_type=MESH,
        )

    between(-1)
    twin_copy.wait()
    first = low == 0
    for side in range(2):
        at = slice(side * half_width, (side + 1) * half_width)
        ours, theirs = own_ref[:, at], twin[:, at]
        wall[(side,) + tuple(bits)] = jnp.concatenate(
            [jnp.where(first, ours, theirs), jnp.where(first, theirs, ours)], axis=0
        ).astype(BF16)
    for i in range(count):
        for q in range(2):
            if i:
                step_copy(q, i - 1).wait_recv()
            step_copy(q, i).start()
        for q in range(2):
            if i:
                pass_copy(q, i - 1).start()
        between(i)
    for q in range(2):
        step_copy(q, count - 1).wait_recv()
        pass_copy(q, count - 1).start()
    for i in range(count):
        for q in range(2):
            step_copy(q, i).wait_send()
            pass_copy(q, i).wait()


def is_me(device):
    return (device[0] == lax.axis_index("expert")) & (device[1] == lax.axis_index("head"))


def hosts(experts):
    at_expert, at_head = lax.axis_index("expert"), lax.axis_index("head")
    part, half, low = where_am_i(experts)
    quarter = experts // 4
    a, b = lax.div(at_expert, 2 * quarter), lax.rem(lax.div(at_expert, quarter), 2)
    out = []
    for k in range(2):
        r = lax.rem(lax.div(at_head, 2) + k, 2)
        row = r * 2 * quarter + a * quarter + lax.rem(at_expert, quarter)
        there = (row, lax.rem(a + b + r, 2) * 2 + low)
        back = (part, lax.rem(half + k, 2) * 2 + low)
        out.append((there, back))
    return out


def start_far_first(experts, copies):
    half = where_am_i(experts)[1]
    at = lax.rem(lax.div(lax.axis_index("head"), 2) + half, 2)
    for turn in range(2):
        for k in range(2):

            @pl.when(lax.rem(at + k + turn, 2) == 1)
            def _(k=k):
                for copy in copies[k]:
                    copy[0]()


def maybe_remote(src, dst, send_sem, recv_sem, device, pieces=1):
    same = is_me(device)
    rows = src.shape[0] // pieces

    def remote(rows_at=None):
        return pltpu.make_async_remote_copy(
            src_ref=src if rows_at is None else src.at[rows_at],
            dst_ref=dst if rows_at is None else dst.at[rows_at],
            send_sem=send_sem,
            recv_sem=recv_sem,
            device_id=device,
            device_id_type=MESH,
        )

    def start():
        @pl.when(same)
        def _():
            pltpu.make_async_copy(src, dst, recv_sem).start()

        @pl.when(jnp.logical_not(same))
        def _():
            for i in range(pieces):
                remote(pl.ds(i * rows, rows)).start()

    def arrived():
        @pl.when(same)
        def _():
            pltpu.make_async_copy(src, dst, recv_sem).wait()

        @pl.when(jnp.logical_not(same))
        def _():
            remote().wait_recv()

    def sent():
        @pl.when(jnp.logical_not(same))
        def _():
            remote().wait_send()

    return start, arrived, sent


def owners_of(experts):
    at_expert, at_head = lax.axis_index("expert"), lax.axis_index("head")
    part, half, low = where_am_i(experts)
    quarter = experts // 4
    x = lax.div(at_head, 2)
    a, b = lax.div(at_expert, 2 * quarter), lax.rem(lax.div(at_expert, quarter), 2)
    rest = a * quarter + lax.rem(at_expert, quarter)
    r = lax.rem(x + a + b, 2)
    return dict(
        slot=lax.rem(x + half, 2),
        beside=(at_expert, (1 - x) * 2 + low),
        direct_to=(part, at_head),
        passed_to=(flipped(experts, part, quarter), at_head),
        direct_from=(r * 2 * quarter + rest, at_head),
        passed_from=((1 - r) * 2 * quarter + rest, at_head),
    )


def reduce_steps(
    all_ref,
    out_ref,
    total,
    last,
    spare,
    pair_sem,
    step_send,
    step_recv,
    last_sem,
    landings,
    between,
):
    at_expert, at_head = lax.axis_index("expert"), lax.axis_index("head")
    low = lax.rem(at_head, 2)
    count = all_ref.ndim - 3
    bits = my_bits(count, lax.div(at_expert * 4 + at_head, 2))
    sibling = (at_expert, at_head + 1 - 2 * low)
    half_width = all_ref.shape[-1]
    cols = parts_of(half_width)
    backwards = list(range(count))[::-1]
    orders = (backwards, [backwards[1], backwards[0]] + backwards[2:])

    def pair_copy(q):
        at = (slice(None),) * count + (slice(None), cols[q])
        return pltpu.make_async_remote_copy(
            src_ref=all_ref.at[(1 - low,) + at],
            dst_ref=total.at[at],
            send_sem=pair_sem.at[q],
            recv_sem=pair_sem.at[2 + q],
            device_id=sibling,
            device_id_type=MESH,
        )

    def step_copy(q, i):
        gone, d = orders[q][:i], orders[q][i]
        full = set(range(count)) - set(gone) - {d}
        at = region(bits, full, d, True) + (slice(None), cols[q])
        return pltpu.make_async_remote_copy(
            src_ref=total.at[at],
            dst_ref=landings[q * count + i],
            send_sem=step_send.at[q, i],
            recv_sem=step_recv.at[q, i],
            device_id=across(bits, low, d),
            device_id_type=MESH,
        )

    for q in range(2):
        pair_copy(q).start()
    for q in range(2):
        at = (slice(None),) * count + (slice(None), cols[q])
        pair_copy(q).wait_recv()
        total[at] = (all_ref[(low,) + at].astype(F32) + total[at].astype(F32)).astype(BF16)
        step_copy(q, 0).start()
    for i in range(count):
        between(i)
        for q in range(2):
            step_copy(q, i).wait_recv()
            gone, d = orders[q][:i], orders[q][i]
            full = set(range(count)) - set(gone) - {d}
            at = region(bits, full) + (slice(None), cols[q])
            added = total[at].astype(F32) + landings[q * count + i][...].astype(F32)
            if i < count - 1:
                total[at] = added.astype(BF16)
                step_copy(q, i + 1).start()
            else:
                last[:, cols[q]] = added
    own_rows = out_ref.shape[0]
    top, bottom = last[0:own_rows, :], last[own_rows:, :]
    first = low == 0
    spare[0] = jnp.where(first, bottom, top)
    last_copy = pltpu.make_async_remote_copy(
        src_ref=spare.at[0],
        dst_ref=spare.at[1],
        send_sem=last_sem.at[0],
        recv_sem=last_sem.at[1],
        device_id=sibling,
        device_id_type=MESH,
    )
    last_copy.start()
    ours = jnp.where(first, top, bottom)
    last_copy.wait()
    theirs = spare[1]
    out_ref[:, 0:half_width] = jnp.where(first, ours, theirs)
    out_ref[:, half_width:] = jnp.where(first, theirs, ours)
    for q in range(2):
        pair_copy(q).wait_send()
        for i in range(count):
            step_copy(q, i).wait_send()


def norm_parts(values):
    centered = values - jnp.mean(values, axis=-1, keepdims=True)
    spread = lax.rsqrt(jnp.mean(centered * centered, axis=-1, keepdims=True) + EPS_NORM)
    return centered * spread, spread


def norm_back(grad, unit, spread, gain):
    scaled = grad * gain
    return spread * (
        scaled
        - jnp.mean(scaled, axis=-1, keepdims=True)
        - unit * jnp.mean(scaled * unit, axis=-1, keepdims=True)
    )


def cut(wall, side, start, stop):
    rows = wall[(side,) + (slice(None),) * (wall.ndim - 2) + (slice(start, stop),)]
    return rows.reshape(-1, stop - start)


def forward_kernel(
    x_ref,
    own_ref,
    wide_in,
    tall_in,
    gy_in,
    inner_ref,
    outer_ref,
    qkv_ref,
    o_ref,
    h_ref,
    n2_ref,
    p_ref,
    out_ref,
    wall_ref,
    w_ref,
    x_out,
    gy_out,
    wide_ref,
    tall_ref,
    small,
    stage,
    masters,
    both_ref,
    held,
    twin,
    wall,
    twin_sem,
    step_send,
    step_recv,
    pass_send,
    pass_recv,
    send_sem,
    recv_sem,
    w_send,
    w_recv,
    own_sem,
    load_sem,
    *,
    experts,
    cap,
):
    width = x_ref.shape[1]
    part, half, low = where_am_i(experts)
    at_expert, at_head = lax.axis_index("expert"), lax.axis_index("head")
    sibling = (at_expert, at_head + 1 - 2 * low)
    count = wall.ndim - 3
    bits = my_bits(count, lax.div(at_expert * 4 + at_head, 2))

    def swap_copy(k):
        return pltpu.make_async_remote_copy(
            src_ref=held.at[k],
            dst_ref=out_ref.at[k],
            send_sem=send_sem.at[k],
            recv_sem=recv_sem.at[k],
            device_id=partner(experts, part, half, low, k),
            device_id_type=MESH,
        )

    pieces = w_send.shape[0] // 2
    piece = 2 * width // pieces

    w_copies = [
        [
            maybe_remote(
                both_ref.at[pl.ds(j * piece, piece)],
                w_ref.at[k, pl.ds(j * piece, piece)],
                w_send.at[k * pieces + j],
                w_recv.at[k * pieces + j],
                there,
                2,
            )
            for j in range(pieces)
        ]
        for k, (there, _) in enumerate(hosts(experts))
    ]
    early = early_parts(experts)
    own_copy = pltpu.make_async_copy(held.at[0], out_ref.at[0], own_sem.at[0])
    wall_copy = pltpu.make_async_copy(wall, wall_ref, own_sem.at[1])

    @pl.when(pl.program_id(0) == 0)
    def _():
        loads = [
            pltpu.make_async_copy(ref, masters.at[pl.ds(j * width, width), :], load_sem.at[j])
            for j, ref in enumerate((inner_ref, outer_ref))
        ]
        for load in loads:
            load.start()
        greet(
            [sibling]
            + [across(bits, low, d) for d in range(count)]
            + [partner(experts, part, half, low, k) for k in range(1, experts)]
            + [device for pair in hosts(experts) for device in pair]
        )

        def send_blocks(blocks):
            rows = gy_out[...].reshape(-1, width)
            for k in blocks:
                held[k] = picked_rows(wide_ref, rows, k, cap)
                (swap_copy(k) if k else own_copy).start()

        def between(i):
            if i < 0:
                route(part, wide_in, tall_in, wide_ref, tall_ref, experts, cap)
            if i == 0:
                for load in loads:
                    load.wait()
                both_ref[...] = masters[...].astype(BF16)
                spread_images(stage, gy_in[...], gy_out)
            if 0 <= i < len(early):
                send_blocks(early[i])
            if i == 1:
                start_far_first(experts, w_copies)
            if i == 2:
                spread_images(stage, x_ref[...], x_out)

        gather_steps(
            own_ref, twin, wall, twin_sem, step_send, step_recv, pass_send, pass_recv, between
        )
        wall_copy.start()
        send_blocks([0])
        small[...] = cut(wall, 0, 2 * width, 2 * width + 128).astype(F32).T

    x = x_out[pl.program_id(0)].astype(F32)
    gain, shift = small[experts : experts + 1, :], small[experts + 1 : experts + 2, :]
    unit, _ = norm_parts(x)
    n1 = (unit * gain + shift).astype(BF16)
    for j in range(3):
        qkv_ref[0, :, j * width : (j + 1) * width] = dot_nn(
            n1, cut(wall, j // 2, (j % 2) * width, (j % 2 + 1) * width)
        ).astype(BF16)
    lane = lax.broadcasted_iota(jnp.int32, (PAD, 128), 1)
    key_at = lax.broadcasted_iota(jnp.int32, (PAD, PAD), 1)
    for pair in range(width // 128):
        q = qkv_ref[0, :, pair * 128 : (pair + 1) * 128]
        k = qkv_ref[0, :, width + pair * 128 : width + (pair + 1) * 128]
        v = qkv_ref[0, :, 2 * width + pair * 128 : 2 * width + (pair + 1) * 128]
        halves = []
        for side in range(2):
            mine = (lane < HD) if side == 0 else (lane >= HD)
            scores = dot_nt(jnp.where(mine, q, jnp.zeros_like(q)), k) * (HD**-0.5)
            scores = jnp.where(key_at < SEQ, scores, -1e30)
            expo = jnp.exp(scores - jnp.max(scores, axis=-1, keepdims=True))
            probs = expo / jnp.sum(expo, axis=-1, keepdims=True)
            halves.append(dot_nn(probs.astype(BF16), v))
        o_ref[0, :, pair * 128 : (pair + 1) * 128] = jnp.where(
            lane < HD, halves[0], halves[1]
        ).astype(BF16)
    h = x + dot_nn(o_ref[0], cut(wall, 1, width, 2 * width))
    h_ref[0] = h
    gain, shift = small[experts + 2 : experts + 3, :], small[experts + 3 : experts + 4, :]
    unit, _ = norm_parts(h)
    n2 = (unit * gain + shift).astype(BF16)
    n2_ref[0] = n2
    logits = dot_nt(small[0:experts, :].astype(BF16), n2)
    expo = jnp.exp(logits - jnp.max(logits, axis=0, keepdims=True))
    p_ref[0] = expo / jnp.sum(expo, axis=0, keepdims=True)

    @pl.when(pl.program_id(0) == pl.num_programs(0) - 1)
    def _():
        for j in range(pieces):
            for k in range(2):
                w_copies[k][j][1]()
        for k in sum(early, []):
            swap_copy(k).wait()
        own_copy.wait()
        wall_copy.wait()
        for j in range(pieces):
            for k in range(2):
                w_copies[k][j][2]()


def expert_kernel(
    wide_ref,
    rows_ref,
    g_ref,
    w_ref,
    router_ref,
    y_ref,
    dr_ref,
    pair_ref,
    x_all,
    g_all,
    held,
    w_all,
    acc,
    y_acc,
    dr_acc,
    x_send,
    x_recv,
    y_sem,
    dr_send,
    dr_recv,
    g_sem,
    w_sem,
    own_sem,
    pair_sem,
    sib_sem,
    ready_sem,
    *,
    experts,
    cap,
    group,
):
    part, half, low = where_am_i(experts)
    at_expert, at_head = lax.axis_index("expert"), lax.axis_index("head")
    sibling = (at_expert, at_head + 1 - 2 * low)
    greet([partner(experts, part, half, low, k) for k in range(1, experts)] + [sibling])
    width = x_all.shape[2]
    slice_width = w_all.shape[2]
    tile = group * cap

    def x_copy(k):
        return pltpu.make_async_remote_copy(
            src_ref=held.at[k],
            dst_ref=x_all.at[k, pl.ds(0, cap), :],
            send_sem=x_send.at[k],
            recv_sem=x_recv.at[k],
            device_id=partner(experts, part, half, low, k),
            device_id_type=MESH,
        )

    def y_copy(k):
        return pltpu.make_async_copy(g_all.at[k], y_ref.at[k], y_sem.at[k])

    def dr_copy(k):
        return pltpu.make_async_remote_copy(
            src_ref=x_all.at[k],
            dst_ref=dr_ref.at[k],
            send_sem=dr_send.at[k],
            recv_sem=dr_recv.at[k],
            device_id=partner(experts, part, half, low, k),
            device_id_type=MESH,
        )

    weights = [
        pltpu.make_async_remote_copy(
            src_ref=w_ref.at[j],
            dst_ref=w_all.at[2 + j],
            send_sem=sib_sem.at[j],
            recv_sem=sib_sem.at[2 + j],
            device_id=sibling,
            device_id_type=MESH,
        )
        for j in range(2)
    ] + [pltpu.make_async_copy(w_ref.at[j], w_all.at[j], w_sem.at[j]) for j in range(2)]
    for copy in weights:
        copy.start()
    g_copy = pltpu.make_async_copy(g_ref, g_all, g_sem)
    g_copy.start()
    rows = rows_ref[...]
    turns = sequence(experts)
    for k in turns:
        if k:
            held[k] = picked_rows(wide_ref, rows, k, cap)
            x_copy(k).start()
    x_all[0, 0:cap, :] = picked_rows(wide_ref, rows, 0, cap)
    acc[...] = jnp.zeros_like(acc)
    g_copy.wait()
    for copy in weights:
        copy.wait()

    def one_tile(t, _):
        base = t * group
        names = [block_at(experts, base + j) for j in range(group)]
        for k in names:

            @pl.when(k > 0)
            def _(k=k):
                x_copy(k).wait_recv()

        x = jnp.concatenate([x_all[k, 0:cap, :] for k in names], axis=0)
        g = jnp.concatenate([g_all[k] for k in names], axis=0)
        logits = dot_nt(x, router_ref[...])
        expo = jnp.exp(logits - jnp.max(logits, axis=-1, keepdims=True))
        probs = expo / jnp.sum(expo, axis=-1, keepdims=True)
        name = lax.broadcasted_iota(jnp.int32, probs.shape, 1)
        gate = jnp.sum(jnp.where(name == part, probs, 0.0), axis=-1, keepdims=True)
        dy = (gate * g.astype(F32)).astype(BF16)
        x_turned, dy_turned = x.T, dy.T

        def first(s):
            w_in = w_all[s, 0:width, :]
            w_out = w_all[s, width : 2 * width, :]
            acts, dus = [], []
            for i in range(0, slice_width, 256):
                u = dot_nn(x, w_in[:, i : i + 256])
                da = dot_nt(dy, w_out[i : i + 256, :])
                root = 0.7978845608028654
                sq = u * u
                th = jnp.tanh(u * (root + (root * 0.044715) * sq))
                plus = 0.5 + 0.5 * th
                acts.append((u * plus).astype(BF16))
                slope = plus + (0.5 * u) * (1.0 - th * th) * (root + (3.0 * root * 0.044715) * sq)
                dus.append((da * slope).astype(BF16))
            return jnp.concatenate(acts, axis=1), jnp.concatenate(dus, axis=1), w_in, w_out

        def second(s, fresh, act, du, w_in, w_out):
            y_part, dr_part = dot_nn(act, w_out), dot_nt(du, w_in)
            y_acc[...] = y_part if fresh else y_acc[...] + y_part
            dr_acc[...] = dr_part if fresh else dr_acc[...] + dr_part
            acc[s, 0] += dot_nn(x_turned, du)
            acc[s, 1] += dot_nn(dy_turned, act)

        order = (2, 3, 0, 1)
        kept = first(order[0])
        for i in range(1, 4):
            fresh = first(order[i])
            second(order[i - 1], i == 1, *kept)
            kept = fresh
        second(order[3], False, *kept)

        y = y_acc[...]
        dgate = jnp.sum(g.astype(F32) * y, axis=-1, keepdims=True)
        dr_low, y_low = dr_acc[...].astype(BF16), (gate * y).astype(BF16)
        for j, k in enumerate(names):
            x_all[k, 0:cap, :] = dr_low[j * cap : (j + 1) * cap, :]
            g_all[k] = y_low[j * cap : (j + 1) * cap, :]
            line = jnp.broadcast_to(dgate[j * cap : (j + 1) * cap, :], (cap, 128))
            if cap % 128:
                line = jnp.concatenate([line, jnp.zeros((128 - cap % 128, 128), F32)], axis=0)
            line = line.T[0:1, :]
            top = line.astype(BF16).astype(F32)
            middle = (line - top).astype(BF16).astype(F32)
            last = line - top - middle
            long = line.shape[1]
            meta = jnp.concatenate([top, middle, last, jnp.zeros((13, long), F32)], axis=0)
            meta = jnp.concatenate([meta, jnp.zeros((16, width - long), F32)], axis=1)
            x_all[k, cap : cap + 16, :] = meta.astype(BF16)

        for k in names:

            @pl.when(k > 0)
            def _(k=k):
                dr_copy(k).start()

            @pl.when(k == 0)
            def _():
                pltpu.make_async_copy(x_all.at[0], dr_ref.at[0], own_sem).start()

            y_copy(k).start()

        return 0

    lax.fori_loop(0, experts // group, one_tile, 0)

    pl.semaphore_signal(ready_sem, inc=1, device_id=sibling, device_id_type=MESH)
    for j in range(2):
        for side in range(2):
            w_all[j, side * width : (side + 1) * width, :] = acc[2 + j, side].astype(BF16)
    pl.semaphore_wait(ready_sem, 1)
    swaps = [
        pltpu.make_async_remote_copy(
            src_ref=w_all.at[j],
            dst_ref=w_all.at[2 + j],
            send_sem=pair_sem.at[j],
            recv_sem=pair_sem.at[2 + j],
            device_id=sibling,
            device_id_type=MESH,
        )
        for j in range(2)
    ]
    for copy in swaps:
        copy.start()
    results = []
    for j in range(2):
        swaps[j].wait()
        for side in range(2):
            at = slice(side * width, (side + 1) * width)
            w_all[2 + j, at, :] = (w_all[2 + j, at, :].astype(F32) + acc[j, side]).astype(BF16)
        results.append(pltpu.make_async_copy(w_all.at[2 + j], pair_ref.at[j], w_sem.at[j]))
        results[-1].start()
    for copy in results:
        copy.wait()

    def settle(k, _):
        x_copy(k).wait_send()
        dr_copy(k).wait()
        y_copy(k).wait()
        return 0

    lax.fori_loop(1, experts, settle, 0)
    y_copy(0).wait()
    pltpu.make_async_copy(x_all.at[0], dr_ref.at[0], own_sem).wait()


def backward_kernel(
    tall_ref,
    gy_ref,
    x_ref,
    h_ref,
    qkv_ref,
    o_ref,
    p_ref,
    wall_ref,
    dr_ref,
    y_ref,
    pair_ref,
    grad_ref,
    out_ref,
    shared_ref,
    back_ref,
    beside_ref,
    small,
    acc,
    small_acc,
    dqkv,
    dp_all,
    y_in,
    send_sem,
    recv_sem,
    own_sem,
    g_send,
    g_recv,
    all_ref,
    total,
    last,
    spare,
    pair_sem,
    step_send,
    step_recv,
    last_sem,
    *landings,
    experts,
    cap,
):
    width = x_ref.shape[2]
    part, half, low = where_am_i(experts)
    step = pl.program_id(0)

    def swap_copy(k):
        return pltpu.make_async_remote_copy(
            src_ref=y_ref.at[k],
            dst_ref=y_in.at[k],
            send_sem=send_sem.at[k],
            recv_sem=recv_sem.at[k],
            device_id=partner(experts, part, half, low, k),
            device_id_type=MESH,
        )

    own_copy = pltpu.make_async_copy(y_ref.at[0], y_in.at[0], own_sem)
    at_expert, at_head = lax.axis_index("expert"), lax.axis_index("head")
    sibling = (at_expert, at_head + 1 - 2 * low)
    count = all_ref.ndim - 3
    bits = my_bits(count, lax.div(at_expert * 4 + at_head, 2))
    ways = owners_of(experts)
    slot_at = ways["slot"]
    direct = maybe_remote(
        pair_ref.at[slot_at],
        back_ref.at[slot_at],
        g_send.at[0],
        g_recv.at[0],
        ways["direct_to"],
        12,
    )
    turns = beside_ref.shape[0]
    piece = beside_ref.shape[1]
    aside = [
        pltpu.make_async_remote_copy(
            src_ref=pair_ref.at[1 - slot_at, pl.ds(j * piece, piece)],
            dst_ref=beside_ref.at[j],
            send_sem=g_send.at[1 + j],
            recv_sem=g_recv.at[1 + j],
            device_id=ways["beside"],
            device_id_type=MESH,
        )
        for j in range(turns)
    ]
    passed = [
        maybe_remote(
            beside_ref.at[j],
            back_ref.at[slot_at, pl.ds(j * piece, piece)],
            g_send.at[1 + turns + j],
            g_recv.at[1 + turns + j],
            ways["passed_to"],
            3,
        )
        for j in range(turns)
    ]

    @pl.when(step == 0)
    def _():
        greet(
            [sibling, ways["beside"]]
            + [across(bits, low, d) for d in range(count)]
            + [partner(experts, part, half, low, k) for k in range(1, experts)]
            + [ways["direct_to"], ways["passed_to"], ways["direct_from"], ways["passed_from"]]
        )
        for j in range(turns):
            aside[j].start()
        direct[0]()
        for k in range(experts - 1, 0, -1):
            swap_copy(k).start()
        own_copy.start()
        small[...] = wall_ref[0, :, 2 * width :].astype(F32).T
        acc[...] = jnp.zeros_like(acc)
        small_acc[...] = jnp.zeros_like(small_acc)

    gy = gy_ref[0].astype(F32)
    h = h_ref[step]
    unit, spread = norm_parts(h)
    gain, shift = small[experts + 2 : experts + 3, :], small[experts + 3 : experts + 4, :]
    n2 = (unit * gain + shift).astype(BF16)
    slot = lax.broadcasted_iota(jnp.int32, (PAD, cap), 1)

    def owners(image, k):
        first = tall_ref[image, :, 0:1] - k * cap
        second = tall_ref[image, :, 1:2] - k * cap
        return ((first == slot) | (second == slot)).astype(F32).astype(BF16)

    dn2 = jnp.zeros((PAD, width), F32)
    for k in range(experts):
        pick = owners(step, k)
        dn2 = dn2 + dot_nn(pick, dr_ref[k, 0:cap, :])
        line = dot_nt(dr_ref[k, cap : cap + 16, 0:cap], pick)
        dp_all[pl.ds(flipped(experts, part, k), 1), :] = (
            line[0:1, :] + line[1:2, :] + line[2:3, :]
        )
    probs = p_ref[0]
    dp = dp_all[...]
    dlogits = (probs * (dp - jnp.sum(dp * probs, axis=0, keepdims=True))).astype(BF16)
    small_acc[0:experts, :] += dot_nn(dlogits, n2)
    dn2 = dn2 + dot_tn(dlogits, small[0:experts, :].astype(BF16))
    small_acc[experts + 2 : experts + 3, :] += jnp.sum(dn2 * unit, axis=0, keepdims=True)
    small_acc[experts + 3 : experts + 4, :] += jnp.sum(dn2, axis=0, keepdims=True)
    dh = gy + norm_back(dn2, unit, spread, gain)
    dh_low = dh.astype(BF16)
    acc[0:width, 3 * width :] += dot_tn(o_ref[0], dh_low)
    do = dot_nt(dh_low, wall_ref[1, :, width : 2 * width]).astype(BF16)

    lane = lax.broadcasted_iota(jnp.int32, (PAD, 128), 1)
    key_at = lax.broadcasted_iota(jnp.int32, (PAD, PAD), 0)
    for pair in range(width // 128):
        q = qkv_ref[0, :, pair * 128 : (pair + 1) * 128]
        k = qkv_ref[0, :, width + pair * 128 : width + (pair + 1) * 128]
        v = qkv_ref[0, :, 2 * width + pair * 128 : 2 * width + (pair + 1) * 128]
        dop = do[:, pair * 128 : (pair + 1) * 128]
        parts = []
        for side in range(2):
            mine = (lane < HD) if side == 0 else (lane >= HD)
            k_mine = jnp.where(mine, k, jnp.zeros_like(k))
            v_mine = jnp.where(mine, v, jnp.zeros_like(v))
            scores = dot_nt(k_mine, q) * (HD**-0.5)
            scores = jnp.where(key_at < SEQ, scores, -1e30)
            expo = jnp.exp(scores - jnp.max(scores, axis=0, keepdims=True))
            prob = expo / jnp.sum(expo, axis=0, keepdims=True)
            dprob = dot_nt(v_mine, dop)
            dscore = prob * (dprob - jnp.sum(dprob * prob, axis=0, keepdims=True))
            dz = (dscore * (HD**-0.5)).astype(BF16)
            parts.append((dot_tn(dz, k), dot_nn(dz, q), dot_nn(prob.astype(BF16), dop)))
        for j in range(3):
            dqkv[:, j * width + pair * 128 : j * width + (pair + 1) * 128] = jnp.where(
                lane < HD, parts[0][j], parts[1][j]
            ).astype(BF16)

    unit, spread = norm_parts(x_ref[0].astype(F32))
    gain, shift = small[experts : experts + 1, :], small[experts + 1 : experts + 2, :]
    n1 = (unit * gain + shift).astype(BF16)
    dn1 = jnp.zeros((PAD, width), F32)
    for j in range(3):
        cols = slice(j * width, (j + 1) * width)
        acc[0:width, cols] += dot_tn(n1, dqkv[:, cols])
        dn1 = dn1 + dot_nt(
            dqkv[:, cols], wall_ref[j // 2, :, (j % 2) * width : (j % 2 + 1) * width]
        )
    small_acc[experts : experts + 1, :] += jnp.sum(dn1 * unit, axis=0, keepdims=True)
    small_acc[experts + 1 : experts + 2, :] += jnp.sum(dn1, axis=0, keepdims=True)
    grad = dh + norm_back(dn1, unit, spread, gain)
    images = tall_ref.shape[0]
    for i in range(images):

        @pl.when(step == i)
        def _(i=i):
            grad_ref[i * SEQ : (i + 1) * SEQ, :] = grad[0:SEQ, :]

    for j in range(turns):

        @pl.when(step == j)
        def _(j=j):
            aside[j].wait_recv()
            passed[j][0]()

    @pl.when(step == pl.num_programs(0) - 1)
    def _():
        blocks = all_ref.shape[1:-1]
        everything = (slice(None),) * len(blocks)
        for j in range(4):
            all_ref[(j // 2,) + everything + (slice((j % 2) * width, (j % 2 + 1) * width),)] = (
                acc[0:width, j * width : (j + 1) * width].astype(BF16).reshape(blocks + (width,))
            )
        rest = (slice(2 * width, 2 * width + 128),)
        all_ref[(0,) + everything + rest] = (
            small_acc[...].T.astype(BF16).reshape(blocks + (128,))
        )
        all_ref[(1,) + everything + rest] = jnp.zeros(blocks + (128,), BF16)

        def one_image(image):
            mixed = h_ref[image]
            for k in range(experts):
                mixed = mixed + dot_nn(owners(image, k), y_in[k])
            acc[image * SEQ : (image + 1) * SEQ, 0:width] = mixed[0:SEQ, :]

        def between(i):
            if i == count - 1:
                for k in range(1, experts):
                    swap_copy(k).wait()
                own_copy.wait()
                for image in range(images):
                    one_image(image)
                out_ref[...] = acc[0 : out_ref.shape[0], 0:width].astype(BF16)

        reduce_steps(
            all_ref,
            shared_ref,
            total,
            last,
            spare,
            pair_sem,
            step_send,
            step_recv,
            last_sem,
            landings,
            between,
        )
        for j in range(turns):
            aside[j].wait_send()
            passed[j][1]()
            passed[j][2]()
        direct[1]()
        direct[2]()


def adam_kernel(*refs, rates, shapes):
    ins, outs = refs[: len(refs) - 24], refs[len(refs) - 24 :]
    inner, outer = ins[0:3], ins[3:6]
    a0, a1, b0, b1 = ins[6:10]
    shared = ins[10:22]
    qkv_grad, router_grad, norm_grad, shared_grad = ins[22:26]

    def put(at, masters, grad, rate):
        new = adam_step(*(m[...] for m in masters), grad, rate)
        for j in range(4):
            outs[at + j][...] = new[j]

    put(16, inner, a0[0].astype(F32) + a1[0].astype(F32), rates[4])
    put(20, outer, (b0[0].astype(F32) + b1[0].astype(F32)).T, rates[5])

    @pl.when(pl.program_id(0) == 0)
    def _():
        proj = shapes
        put(0, shared[0:3], qkv_grad[...], rates[0])
        put(4, shared[3:6], shared_grad[:, proj[0] : proj[1]], rates[1])
        put(8, shared[6:9], router_grad[...], rates[2])
        put(12, shared[9:12], norm_grad[...], rates[3])


def on_device(
    expert_axis,
    block_input,
    output_grad,
    routes,
    qkv_master,
    qkv_mean,
    qkv_square,
    proj_master,
    proj_mean,
    proj_square,
    router_master,
    router_mean,
    router_square,
    norm_master,
    norm_mean,
    norm_square,
    inner_master,
    inner_mean,
    inner_square,
    outer_master,
    outer_mean,
    outer_square,
):
    row_count, width = block_input.shape
    heads = width // HD
    images = row_count // SEQ
    tokens = images * PAD
    experts = router_master.shape[1]
    own_rows = qkv_master.shape[0]
    bound = row_count * 16 // (5 * experts) + 1
    cap = -(-bound // 16) * 16
    group = max(1, min(experts, 640 // cap // 2 * 2))
    while experts % group:
        group = group - 1
    slice_width = inner_master.shape[2]
    vmem = pl.BlockSpec(memory_space=pltpu.VMEM)
    smem = pl.BlockSpec(memory_space=pltpu.SMEM)
    anywhere = pl.BlockSpec(memory_space=pl.ANY)
    struct = jax.ShapeDtypeStruct

    qkv_own = qkv_master.reshape(own_rows, heads, 3, HD).transpose(0, 2, 1, 3)
    qkv_own = qkv_own.reshape(own_rows, 3 * width)
    wall_own = jnp.concatenate(
        [
            qkv_own[:, : 2 * width],
            router_master,
            norm_master.T,
            jnp.zeros((own_rows, 128 - experts - 4), F32),
            qkv_own[:, 2 * width :],
            proj_master,
            jnp.zeros((own_rows, 128), F32),
        ],
        axis=1,
    )
    half_width = 2 * width + 128
    count = (width // own_rows).bit_length() - 2
    block = (2,) * count + (2 * own_rows, half_width)

    tall = jnp.pad(
        routes.reshape(images, SEQ, 2), ((0, 0), (0, PAD - SEQ), (0, 0)), constant_values=-1
    ).reshape(tokens, 2)
    dma = pltpu.SemaphoreType.DMA

    def image_spec(*dims):
        return pl.BlockSpec((1,) + dims, lambda i: (i,) + (0,) * len(dims))

    def whole_spec(*dims, once=True):
        mode = dict(pipeline_mode=pl.Buffered(1)) if once else {}
        return pl.BlockSpec(dims, lambda i: (0,) * len(dims), **mode)

    qkv, attended, middle, second, probs, g_blocks, wall, w_all, x, gy, wide_slots, tall_slots = (
        pl.pallas_call(
            functools.partial(forward_kernel, experts=experts, cap=cap),
            grid=(images,),
            out_shape=(
                struct((images, PAD, 3 * width), BF16),
                struct((images, PAD, width), BF16),
                struct((images, PAD, width), F32),
                struct((images, PAD, width), BF16),
                struct((images, experts, PAD), F32),
                struct((experts, cap, width), BF16),
                struct((2,) + block, BF16),
                struct((2, 2 * width, slice_width), BF16),
                struct((images, PAD, width), BF16),
                struct((images, PAD, width), BF16),
                struct((2, tokens), jnp.int32),
                struct((images, PAD, 2), jnp.int32),
            ),
            in_specs=[
                whole_spec(row_count, width),
                whole_spec(*wall_own.shape),
                whole_spec(2, tokens),
                whole_spec(tokens, 2),
                whole_spec(row_count, width),
                anywhere,
                anywhere,
            ],
            out_specs=(
                image_spec(PAD, 3 * width),
                image_spec(PAD, width),
                image_spec(PAD, width),
                image_spec(PAD, width),
                image_spec(experts, PAD),
                anywhere,
                anywhere,
                anywhere,
                whole_spec(images, PAD, width, once=False),
                whole_spec(images, PAD, width, once=False),
                whole_spec(2, tokens, once=False),
                whole_spec(images, PAD, 2, once=False),
            ),
            scratch_shapes=[
                pltpu.VMEM((128, width), F32),
                pltpu.VMEM((tokens, width), F32),
                pltpu.VMEM((2 * width, slice_width), F32),
                pltpu.VMEM((2 * width, slice_width), BF16),
                pltpu.VMEM((experts, cap, width), BF16),
                pltpu.VMEM(wall_own.shape, F32),
                pltpu.VMEM((2,) + block, BF16),
                dma((2,)),
            ]
            + [dma((2, count))] * 4
            + [dma((experts,))] * 2
            + [dma((8,))] * 2
            + [dma((2,))] * 2,
            compiler_params=params(collective_id=0, has_side_effects=True),
            cost_estimate=cost(120),
            name="forward",
        )(
            block_input,
            wall_own,
            tall.T,
            tall,
            output_grad,
            inner_master.reshape(width, slice_width),
            outer_master.reshape(slice_width, width),
        )
    )
    wall = wall.reshape(2, width, half_width)

    router_low = wall[0, :, 2 * width : 2 * width + experts].T
    y_blocks, dr_blocks, grad_pair = pl.pallas_call(
        functools.partial(expert_kernel, experts=experts, cap=cap, group=group),
        out_shape=(
            struct((experts, cap, width), BF16),
            struct((experts, cap + 16, width), BF16),
            struct((2, 2 * width, slice_width), BF16),
        ),
        in_specs=[vmem, vmem, anywhere, anywhere, vmem],
        out_specs=[anywhere] * 3,
        scratch_shapes=[
            pltpu.VMEM((experts, cap + 16, width), BF16),
            pltpu.VMEM((experts, cap, width), BF16),
            pltpu.VMEM((experts, cap, width), BF16),
            pltpu.VMEM((4, 2 * width, slice_width), BF16),
            pltpu.VMEM((4, 2, width, slice_width), F32),
            pltpu.VMEM((group * cap, width), F32),
            pltpu.VMEM((group * cap, width), F32),
        ]
        + [dma((experts,))] * 5
        + [dma, dma((4,)), dma, dma((4,)), dma((4,)), pltpu.SemaphoreType.REGULAR],
        compiler_params=params(collective_id=1, has_side_effects=True),
        cost_estimate=cost(140),
        name="experts",
    )(
        wide_slots,
        second.reshape(tokens, width),
        g_blocks,
        w_all,
        router_low,
    )

    landings = [
        pltpu.VMEM((2,) * (count - 1 - i) + (2 * own_rows, c.stop - c.start), BF16)
        for c in parts_of(half_width)
        for i in range(count)
    ]
    input_grad, block_output, shared_own, grad_back, _ = pl.pallas_call(
        functools.partial(backward_kernel, experts=experts, cap=cap),
        grid=(images,),
        out_shape=(
            struct((row_count, width), F32),
            struct((row_count, width), BF16),
            struct((own_rows, 2 * half_width), F32),
            struct((2, 2 * width, slice_width), BF16),
            struct((images, 2 * width // images, slice_width), BF16),
        ),
        in_specs=[
            whole_spec(images, PAD, 2),
            image_spec(PAD, width),
            image_spec(PAD, width),
            whole_spec(images, PAD, width),
            image_spec(PAD, 3 * width),
            image_spec(PAD, width),
            image_spec(experts, PAD),
            whole_spec(2, width, half_width),
            whole_spec(experts, cap + 16, width),
            anywhere,
            anywhere,
        ],
        out_specs=(
            whole_spec(row_count, width),
            whole_spec(row_count, width),
            whole_spec(own_rows, 2 * half_width),
            anywhere,
            anywhere,
        ),
        scratch_shapes=[
            pltpu.VMEM((128, width), F32),
            pltpu.VMEM((max(width, row_count + 7 & -8), 4 * width), F32),
            pltpu.VMEM((128, width), F32),
            pltpu.VMEM((PAD, 3 * width), BF16),
            pltpu.VMEM((experts, PAD), F32),
            pltpu.VMEM((experts, cap, width), BF16),
            dma((experts,)),
            dma((experts,)),
            dma,
            dma((1 + 2 * images,)),
            dma((1 + 2 * images,)),
            pltpu.VMEM((2,) + block, BF16),
            pltpu.VMEM(block, BF16),
            pltpu.VMEM((2 * own_rows, half_width), F32),
            pltpu.VMEM((2, own_rows, half_width), F32),
            dma((4,)),
            dma((2, count)),
            dma((2, count)),
            dma((2,)),
        ]
        + landings,
        compiler_params=params(collective_id=2, has_side_effects=True),
        cost_estimate=cost(120),
        name="backward",
    )(tall_slots, gy, x, middle, qkv, attended, probs, wall, dr_blocks, y_blocks, grad_pair)

    qkv_owned = jnp.concatenate(
        [shared_own[:, : 2 * width], shared_own[:, half_width : half_width + width]], axis=1
    )
    qkv_owned = qkv_owned.reshape(own_rows, 3, heads, HD).transpose(0, 2, 1, 3)
    qkv_owned = qkv_owned.reshape(own_rows, 3 * width)
    small_owned = shared_own[:, 2 * width : 2 * width + experts + 4].T
    small_owned = [small_owned[:experts], small_owned[experts:]]

    rates = (
        2.0 * width ** (-0.5),
        2.0 * (width // 16) ** (-0.5),
        2.0 * (4 * width) ** (-0.5),
        NORM_RATE,
        2.0 * width ** (-0.5),
        2.0 * max(1, FF * 4 // (experts * experts)) ** (-0.5),
    )
    step_rows = width // 2 if width % 256 == 0 else 128

    def rows_spec(cols):
        return pl.BlockSpec((step_rows, cols), lambda i: (i, 0))

    shared = [
        qkv_master,
        qkv_mean,
        qkv_square,
        proj_master,
        proj_mean,
        proj_square,
        router_master.T,
        router_mean.T,
        router_square.T,
        norm_master,
        norm_mean,
        norm_square,
    ]
    inner = [v.reshape(width, slice_width) for v in (inner_master, inner_mean, inner_square)]
    outer = [v.reshape(slice_width, width) for v in (outer_master, outer_mean, outer_square)]
    state = []
    for v in shared[::3] + [inner[0], outer[0]]:
        state += [struct(v.shape, t) for t in (F32, F32, F32, BF16)]
    new = pl.pallas_call(
        functools.partial(
            adam_kernel,
            rates=rates,
            shapes=(half_width + width, half_width + 2 * width),
        ),
        grid=(width // step_rows,),
        out_shape=state,
        in_specs=[rows_spec(slice_width)] * 3
        + [rows_spec(width)] * 3
        + [
            pl.BlockSpec((1, step_rows, slice_width), functools.partial(lambda k, i: (k, i, 0), k))
            for k in range(2)
        ]
        + [
            pl.BlockSpec((1, width, step_rows), functools.partial(lambda k, i: (k, 1, i), k))
            for k in range(2)
        ]
        + [whole_spec(*v.shape) for v in shared + [qkv_owned] + small_owned + [shared_own]],
        out_specs=[whole_spec(*v.shape, once=False) for v in state[:16]]
        + [rows_spec(slice_width)] * 4
        + [rows_spec(width)] * 4,
        compiler_params=params(),
        cost_estimate=cost(15),
        name="adam",
    )(*inner, *outer, *([grad_back] * 4), *shared, qkv_owned, *small_owned, shared_own)
    return (
        block_output,
        input_grad,
        *new[:8],
        *(v.T for v in new[8:12]),
        *new[12:16],
        *(v[None] for v in new[16:]),
    )


def solution(mesh):
    rows = P(AXES, None)
    cols = P(None, AXES)
    inner = P("expert", None, "head")
    outer = P("expert", "head", None)
    in_specs = (rows,) * 12 + (cols,) * 3 + (inner,) * 3 + (outer,) * 3
    out_specs = (rows,) * 14 + (cols,) * 4 + (inner,) * 4 + (outer,) * 4
    return jax.shard_map(
        functools.partial(on_device, mesh.shape["expert"]),
        mesh=mesh,
        in_specs=in_specs,
        out_specs=out_specs,
        check_vma=False,
    )
```
